128 devices in a mesh: dp: 32 (over x, y, core), heads: 4 (over z).
Axes of the slice: x: 4, y: 4, z: 4, core: 2. Of those that a mesh axis runs over, the one named last changes fastest.
Arguments:
- inputs: bfloat16 [96, 512, 768], P('dp', 'heads'), may hold values from -6 to 6
- key_mask: int32 [96, 512], P('dp'), may hold values from 0 to 1, as said below
- lengths: int32 [96], P('dp'), may hold values from 8 to 512, as said below
- cotangent: bfloat16 [96, 512, 768], P('dp', 'heads'), may hold values from -6 to 6
- query_weight: bfloat16 [768, 768], P(None, 'heads'), may hold values from -0.3125 to 0.3125
- w_key: bfloat16 [768, 768], P(None, 'heads'), may hold values from -0.21875 to 0.21875
- value_weight: bfloat16 [768, 768], P(None, 'heads'), may hold values from -0.21875 to 0.21875
- w_out: bfloat16 [768, 768], replicated, may hold values from -1.25 to 1.25
- w_inner: bfloat16 [768, 3072], replicated, may hold values from -0.21875 to 0.21875
- w_outer: bfloat16 [3072, 768], replicated, may hold values from -0.109375 to 0.109375
- gain_one: float32 [768], replicated, may hold values from 0.1 to 1.9
- shift_one: float32 [768], replicated, may hold values from -3 to 3
- gain_two: float32 [768], replicated, may hold values from 0.1 to 1.9
- shift_two: float32 [768], replicated, may hold values from -3 to 3
- down_query: bfloat16 [768, 8], replicated, may hold values from -0.21875 to 0.21875
- query_up_map: bfloat16 [8, 768], P(None, 'heads'), may hold values from -1 to 1
- down_value: bfloat16 [768, 8], replicated, may hold values from -0.21875 to 0.21875
- value_up_map: bfloat16 [8, 768], P(None, 'heads'), may hold values from -1 to 1
Outputs:
- activation: bfloat16 [96, 512, 768], P('dp', 'heads')
- input_grad: float32 [96, 512, 768], P('dp', 'heads')
- grad_down_query: float32 [768, 8], replicated
- grad_up_query: float32 [8, 768], P(None, 'heads')
- grad_down_value: float32 [768, 8], replicated
- grad_up_value: float32 [8, 768], P(None, 'heads')
The draws below stay inside these ranges and needn't reach their ends.
Inputs may be any that keep to these rules, and one draw needn't show every extreme that they name: `lengths`: in each aligned block of 3 sentences one sentence, drawn from the seed, has length 512. `key_mask`: 1 only at positions below the sentence's length; position 0 is always 1.
All inputs are finite; a program needn't handle non-finite values.
Results may differ from the reference program's by a relative error of at most 0.019.
The reference program's roundings to bfloat16 on the way count: a program that leaves them out, or rounds other values in their place, can miss the bound.
Values may be sent and summed in bfloat16 or wider, within the bound.
A program may use at most 128 MiB of HBM per device.

```python
import math
import jax
import jax.numpy as jnp
from jax import lax

D = 768
HD = 64
FF = 3072
R = 8
L = 512
BATCH_DEV = 3
BATCH = 96


def shared_lengths(key):
    base = jax.random.fold_in(key, 11)
    first_key, second_key = jax.random.split(base)
    sizes = jax.random.randint(first_key, (BATCH,), min(8, L), L + 1)
    chosen = jax.random.randint(second_key, (BATCH // BATCH_DEV,), 0, BATCH_DEV)
    slot_index = jnp.arange(BATCH) % BATCH_DEV
    owner = chosen[jnp.arange(BATCH) // BATCH_DEV]
    return jnp.where(slot_index == owner, L, sizes).astype(jnp.int32)


def draw_lengths(key, part):
    sizes = shared_lengths(key)
    return sizes


def draw_key_mask(key, part):
    sizes = shared_lengths(key)
    key = jax.random.fold_in(key, 5)
    drops = jax.random.randint(key, (BATCH, L), 0, 8)
    position = jnp.arange(L)[None, :]
    kept = (position < sizes[:, None]) & ((drops != 0) | (position == 0))
    return kept.astype(jnp.int32)


def steps_of(rng, extent, cuts, low, high):
    gain, own = 1.0, jax.random.fold_in(rng, 6)
    for dim, parts in cuts:
        heights = jnp.exp(jax.random.uniform(jax.random.fold_in(own, dim), (parts,), jnp.float32, low / len(cuts), high / len(cuts)))
        gain = gain * jnp.repeat(heights, extent[dim] // parts).reshape([-1 if axis == dim else 1 for axis in range(len(extent))])
    return gain


def gaussian(key, extent, scale, reach, cuts=(), kind=jnp.bfloat16):
    entries = jax.random.normal(key, extent, jnp.float32) * scale
    if len(cuts) > 0:
        entries = steps_of(key, extent, cuts, -0.22, 0.18) * entries
    return jnp.clip(entries, min=-reach, max=reach).astype(kind)


def setup_inputs(seed: int = 0) -> dict:
    key_of = jax.random.split(jax.random.key(seed), 19)
    inputs = gaussian(key_of[0], (BATCH, L, D), 1.0, 6.0, ((0, 32), (1, 4)))
    key_mask = draw_key_mask(jax.random.fold_in(key_of[18], 71), 0)
    lengths = draw_lengths(jax.random.fold_in(key_of[18], 71), 0)
    cotangent = gaussian(key_of[3], (BATCH, L, D), 1.0, 6.0, ((0, 32), (1, 4)))
    query_weight = gaussian(key_of[4], (D, D), (D // 2) ** -0.5, 0.3125, ((1, 4),))
    w_key = gaussian(key_of[5], (D, D), D ** -0.5, 0.21875, ((1, 4),))
    value_weight = gaussian(key_of[6], (D, D), D ** -0.5, 0.21875, ((1, 4),))
    w_out = gaussian(key_of[7], (D, D), (D // 32) ** -0.5, 1.25)
    w_inner = gaussian(key_of[8], (D, FF), D ** -0.5, 0.21875)
    w_outer = gaussian(key_of[9], (FF, D), FF ** -0.5, 0.109375)
    gain_one = jnp.clip(1.0 + 0.18 * jax.random.normal(key_of[10], (D,), jnp.float32), 0.1, 1.9)
    shift_one = gaussian(key_of[11], (D,), 0.5, 3.0, (), jnp.float32)
    gain_two = jnp.clip(1.0 + 0.18 * jax.random.normal(key_of[12], (D,), jnp.float32), 0.1, 1.9)
    shift_two = gaussian(key_of[13], (D,), 0.5, 3.0, (), jnp.float32)
    down_query = gaussian(key_of[14], (D, R), D ** -0.5, 0.21875)
    query_up_map = gaussian(key_of[15], (R, D), (4 * R) ** -0.5, 1.0, ((1, 4),))
    down_value = gaussian(key_of[16], (D, R), D ** -0.5, 0.21875)
    value_up_map = gaussian(key_of[17], (R, D), (4 * R) ** -0.5, 1.0, ((1, 4),))
    return dict(inputs=inputs, key_mask=key_mask, lengths=lengths, cotangent=cotangent, query_weight=query_weight, w_key=w_key, value_weight=value_weight, w_out=w_out, w_inner=w_inner, w_outer=w_outer, gain_one=gain_one, shift_one=shift_one, gain_two=gain_two, shift_two=shift_two, down_query=down_query, query_up_map=query_up_map, down_value=down_value, value_up_map=value_up_map)


@jax.custom_vjp
def low(v):
    return lax.optimization_barrier(v.astype(jnp.bfloat16)).astype(jnp.float32)

@jax.custom_vjp
def low_back(v):
    return v

def low_keep(v):
    return (low(v), None)

def low_pass(kept, grad):
    return (grad,)

def back_keep(v):
    return (v, None)

def back_low(kept, grad):
    return (low(grad),)
low.defvjp(low_keep, low_pass)
low_back.defvjp(back_keep, back_low)
adapter_scale = 2.0
highest = lax.Precision.HIGHEST

def matrix_product(left, right):
    return jnp.matmul(left, right, precision=highest)

def rounded_result(value):
    return low(low_back(value))

def layer_norm(hidden, scale_gain, shift_bias):
    center = hidden - lax.optimization_barrier(jnp.mean(hidden, axis=-1, keepdims=True))
    spread = lax.optimization_barrier(jnp.mean(center * center, axis=-1, keepdims=True))
    return center * lax.rsqrt(spread + 1e-05) * scale_gain + shift_bias

def attend(pieces):
    query_rows, key_rows, value_matrix_rows, key_keep = pieces
    length = query_rows.shape[0]
    head_count = query_rows.shape[1] // HD
    query_rows = query_rows.reshape(length, head_count, HD)
    key_rows = key_rows.reshape(length, head_count, HD)
    value_matrix_rows = value_matrix_rows.reshape(length, head_count, HD)
    scores = jnp.einsum('qhd,khd->hqk', query_rows, key_rows, precision=highest) * (1.0 / math.sqrt(HD))
    scores = low_back(scores)
    scores = jnp.where(key_keep[None, None, :] > 0, scores, -1e+30)
    row_max = lax.optimization_barrier(jnp.max(scores, axis=-1, keepdims=True))
    raised = jnp.exp(scores - row_max)
    attention = raised / lax.optimization_barrier(jnp.sum(raised, axis=-1, keepdims=True))
    context = jnp.einsum('hqk,khd->qhd', low(attention), value_matrix_rows, precision=highest)
    return context.reshape(length, head_count * HD)

def forward(block_data, down_query, query_up_map, down_value, value_up_map, frozen, key_keep):
    query_weight, w_key, value_weight, w_out, w_inner, w_outer, gain_one, shift_one, gain_two, shift_two = frozen
    seq_count, length, features = block_data.shape
    flattened_rows = block_data.reshape(seq_count * length, features)
    query_middle_rank = rounded_result(matrix_product(flattened_rows, down_query))
    value_middle_rank = rounded_result(matrix_product(flattened_rows, down_value))
    query_rows = rounded_result(matrix_product(flattened_rows, query_weight) + adapter_scale * matrix_product(query_middle_rank, query_up_map))
    key_rows = rounded_result(matrix_product(flattened_rows, w_key))
    value_matrix_rows = rounded_result(matrix_product(flattened_rows, value_weight) + adapter_scale * matrix_product(value_middle_rank, value_up_map))
    layout = (seq_count, length, features)
    context = lax.map(jax.checkpoint(attend), (query_rows.reshape(layout), key_rows.reshape(layout), value_matrix_rows.reshape(layout), key_keep))
    context = rounded_result(context.reshape(seq_count * length, features))
    attended = low_back(matrix_product(context, w_out))
    normed_one = layer_norm(flattened_rows + attended, gain_one, shift_one)
    inner_pre = low_back(matrix_product(low(normed_one), w_inner))
    active = low(jax.nn.gelu(inner_pre, approximate=False))
    branch_out = low_back(matrix_product(active, w_outer))
    return layer_norm(normed_one + branch_out, gain_two, shift_two).reshape(layout)

def reference(inputs, key_mask, lengths, cotangent, query_weight, w_key, value_weight, w_out, w_inner, w_outer, gain_one, shift_one, gain_two, shift_two, down_query, query_up_map, down_value, value_up_map):
    frozen = tuple((weight.astype(jnp.float32) for weight in (query_weight, w_key, value_weight, w_out, w_inner, w_outer, gain_one, shift_one, gain_two, shift_two)))
    adapters = tuple((weight.astype(jnp.float32) for weight in (down_query, query_up_map, down_value, value_up_map)))
    seq_block = math.gcd(BATCH, max(1, 4096 // L))
    blocks = BATCH // seq_block
    position = jnp.arange(L, dtype=jnp.int32)
    row_valid = (position[None, :] < lengths[:, None]).astype(jnp.float32)
    tangent = cotangent.astype(jnp.float32) * row_valid[:, :, None]

    def to_blocks(source):
        return source.reshape((blocks, seq_block) + source.shape[1:])

    def one_block(totals, pieces):
        block_in, block_keep, block_tangent = pieces

        def block_forward(block_data, first_down, first_up, second_down, second_up):
            return forward(block_data, first_down, first_up, second_down, second_up, frozen, block_keep)
        result, pullback = jax.vjp(block_forward, block_in.astype(jnp.float32), *adapters)
        gradients = pullback(block_tangent)
        totals = tuple((total + piece for total, piece in zip(totals, gradients[1:])))
        return (totals, (result.astype(jnp.bfloat16), gradients[0]))
    zero_sums = tuple((jnp.zeros_like(weight) for weight in adapters))
    totals, (activation, input_grad) = lax.scan(one_block, zero_sums, (to_blocks(inputs), to_blocks(key_mask), to_blocks(tangent)))
    return (activation.reshape(BATCH, L, D), input_grad.reshape(BATCH, L, D), totals[0], totals[1], totals[2], totals[3])
```

```python
import functools

import jax
import jax.numpy as jnp
from jax import lax
from jax.experimental import pallas as pl
from jax.experimental.pallas import tpu as pltpu
from jax.sharding import Mesh
from jax.sharding import PartitionSpec as P

BF, F32 = jnp.bfloat16, jnp.float32
S, D, FF, HD, G = 512, 768, 3072, 64, 4
B, Q = 3, 128
GW = 640
C = 256
NT = (((1,), (1,)), ((), ()))
DP = ("dp_0", "dp_1", "dp_2")
MESH = pl.DeviceIdType.MESH
LANES = ((0, 384), (384, 256))


def nn(a, b):
    return jnp.dot(a, b, preferred_element_type=F32)


def nt(a, b):
    return lax.dot_general(a, b, NT, preferred_element_type=F32)


def project(g, x, wg, up, bias, knat, vnat, yt):
    xv = x[...]
    tail = nn(xv, wg[g, :, 384:GW])
    lane = lax.broadcasted_iota(jnp.int32, (S, 256), 1)
    kb = jnp.where(lane == 255, bias[...], tail).astype(BF)
    knat[g] = kb
    qv = nn(xv, wg[g, :, 0:384]) + nn(kb[:, 128:256], up[g])
    lane2 = lax.broadcasted_iota(jnp.int32, (S, 384), 1)
    qvb = qv.astype(BF)
    vnat[g] = qvb[:, 128:384]
    qvs = jnp.where(lane2 < 192, qvb * 0.125, qvb).astype(BF)
    yt[g, 0:384, :] = qvs.T
    yt[g, 384:GW, :] = kb.T


def pad_rows(piece, before, total):
    parts = []
    if before:
        parts.append(jnp.zeros((before, S), BF))
    parts.append(piece)
    after = total - before - piece.shape[0]
    if after:
        parts.append(jnp.zeros((after, S), BF))
    return jnp.concatenate(parts, axis=0)


def attend(g, knat, yt, sscr, p, rl, ctxt):
    one_row = (lax.broadcasted_iota(jnp.int32, (64, S), 0) == 63).astype(BF)
    ones = jnp.ones((16, S), BF)
    kb = knat[g]
    for j in range(3):
        rhs = jnp.concatenate([pad_rows(yt[g, 64 * j : 64 * j + 64, :], 64 * j, 192), one_row], axis=0)
        for half in range(2):
            cols = slice(256 * half, 256 * half + 256)
            s = nn(kb, rhs[:, cols])
            sscr[j, half] = s
            m = jnp.max(s, axis=0, keepdims=True)
            p[g * 3 + j, :, cols] = jnp.exp(sscr[j, half] - m).astype(BF)
        vt = jnp.concatenate([yt[g, 192 + 64 * j : 256 + 64 * j, :], ones], axis=0)
        ot = nn(vt, p[g * 3 + j])
        rinv = 1.0 / ot[64:65]
        rl[g * 3 + j] = rinv
        ctxt[g, 64 * j : 64 * j + 64, :] = (ot[0:64] * rinv).astype(BF)


def attend_back(g, vnat, yt, p, rl, ctxt, dot_ref, dsscr, dyt):
    vb = vnat[g]
    for j in range(3):
        h = g * 3 + j
        rows = slice(64 * j, 64 * j + 64)
        do = (dot_ref[g, rows, :] * rl[h]).astype(BF)
        dsum = jnp.sum(do.astype(F32) * ctxt[g, rows, :].astype(F32), axis=0, keepdims=True)
        rhs = pad_rows(do, 64 + 64 * j, 256)
        for half in range(2):
            cols = slice(256 * half, 256 * half + 256)
            dp = nn(vb, rhs[:, cols])
            dsscr[j, :, cols] = (p[h, :, cols].astype(F32) * (dp - dsum[:, cols])).astype(BF)
        dyt[g, 192 + 64 * j : 256 + 64 * j, :] = nt(do, p[h]).astype(BF)
        ds = dsscr[j]
        dyt[g, 384 + 64 * j : 448 + 64 * j, :] = nt(yt[g, rows, :], ds).astype(BF)
        dyt[g, rows, :] = (nn(yt[g, 384 + 64 * j : 448 + 64 * j, :], ds) * 0.125).astype(BF)


def gelu_pair(v):
    e = jnp.exp(v * v * -0.5)
    t = 1.0 / (1.0 + 0.23164189 * jnp.abs(v))
    tail = t * (0.127414796 + t * (-0.142248368 + t * (0.7107068705 + t * (-0.7265760135 + t * 0.5307027145)))) * e
    cdf = jnp.where(v >= 0.0, 1.0 - tail, tail)
    return v * cdf, cdf + v * (e * 0.3989422804)


def norm(h):
    mean = jnp.mean(h, axis=-1, keepdims=True)
    c = h - mean
    r = lax.rsqrt(jnp.mean(c * c, axis=-1, keepdims=True) + 1e-5)
    return c * r, r


def norm_back(n, xhat, r):
    return r * (n - jnp.mean(n, axis=-1, keepdims=True) - xhat * jnp.mean(n * xhat, axis=-1, keepdims=True))


def remote(src, dst, send, recv, **where):
    return pltpu.make_async_remote_copy(
        src_ref=src, dst_ref=dst, send_sem=send, recv_sem=recv, device_id=where, device_id_type=MESH
    )


def layer(
    inputs, cot, kmask, lengths, wq, wk, wv, w_out, w_inner, w_outer, g1, b1, g2, b2, dq, uq, dv, uv,
    act_out, ig_out, gd_out, gu_out,
    x, ct, wqs, wks, wvs, wo, wi, wt, wg, up, act, igb,
    bias, knat, vnat, yt, sscr, p, rl, ctxt, xhat1, r1s, n1b, dact, acc, dot_ref, dsscr, dyt, gnb,
    msg, redz, redc, redx, redy, gdp,
    lsem, xsem, csem, wsem, usem, w1, w2, w3, asem, isem, gz, gc, gx, gy, gf,
):
    ix, iy, ic, iz = (lax.axis_index(a) for a in ("dp_0", "dp_1", "dp_2", "heads"))
    rank = lax.rem(iz + 2 * ic, 4)
    owner = rank < 3
    mine = jnp.minimum(rank, 2)

    def z_of(r):
        return lax.rem(r + 2 * ic, 4)

    def turn(i, by):
        return lax.rem(i + by, 4)

    loads = [
        pltpu.make_async_copy(wq, wqs, lsem.at[0]),
        pltpu.make_async_copy(wv, wvs, lsem.at[1]),
        pltpu.make_async_copy(wk, wks, lsem.at[2]),
    ]
    for c in loads:
        c.start()
    late = [pltpu.make_async_copy(w_inner, wi, lsem.at[3]), pltpu.make_async_copy(w_outer, wt, lsem.at[4])]
    for k in range(G):
        at = pl.multiple_of(turn(iz, k) * 192, 192)
        late.append(pltpu.make_async_copy(w_out.at[pl.ds(at, 192)], wo.at[pl.ds(192 * k, 192)], lsem.at[5 + k]))

    barrier = pltpu.get_barrier_semaphore()
    peers = [{"dp_2": 1 - ic}]
    for i in (1, 2, 3):
        peers += [{"heads": turn(iz, i)}, {"dp_0": turn(ix, i)}, {"dp_1": turn(iy, i)}]
    for where in peers:
        pl.semaphore_signal(barrier, inc=1, device_id=where, device_id_type=MESH)
    pl.semaphore_wait(barrier, 10)

    def slot(ref, r):
        return ref.at[pl.ds(pl.multiple_of(r * Q, Q), Q)]

    def spread(src, dst, sem):
        for j in range(B):
            @pl.when(rank != j)
            def _():
                remote(src.at[j], slot(dst, rank), sem.at[0, j], sem.at[1, rank], heads=z_of(j)).start()

            @pl.when(rank == j)
            def _():
                pltpu.make_async_copy(src.at[j], slot(dst, rank), sem.at[1, j]).start()

    def spread_wait(src, dst, sem):
        @pl.when(owner)
        def _():
            for r in range(4):
                pltpu.make_async_copy(src.at[0], dst.at[pl.ds(r * Q, Q)], sem.at[1, r]).wait()

    def spread_end(src, dst, sem):
        for j in range(B):
            @pl.when(rank != j)
            def _():
                remote(src.at[j], slot(dst, rank), sem.at[0, j], sem.at[1, rank], heads=z_of(j)).wait_send()

    spread(inputs, x, xsem)

    for c in loads:
        c.wait()
    wg[0] = jnp.concatenate(
        [wqs[...], wvs[...], wks[...], dq[...], dv[...], jnp.zeros((D, GW - 592), BF)], axis=1
    )
    up[:, 0:64, :] = jnp.zeros((G, 64, 384), BF)
    up[:, 80:128, :] = jnp.zeros((G, 48, 384), BF)
    zero8 = jnp.zeros((8, 192), F32)
    both = jnp.concatenate(
        [
            jnp.concatenate([uq[...].astype(F32), zero8], axis=1),
            jnp.concatenate([zero8, uv[...].astype(F32)], axis=1),
        ],
        axis=0,
    )
    up[0, 64:80, :] = (2.0 * both).astype(BF)
    rows0 = jnp.where(ic == 0, 192 * iy + 48 * ix, 192 * ix + 48 * iy)
    rows0 = pl.multiple_of(rows0, 48)

    def part(c, k, at, count):
        return wg.at[k, pl.ds(at, count), pl.ds(*LANES[c])]

    def over_z(c):
        return [
            remote(part(c, 0, rows0, 48), part(c, 4 - i, rows0, 48), wsem.at[0, i], wsem.at[1, 4 - i],
                   heads=turn(iz, i))
            for i in (1, 2, 3)
        ]

    def first(c):
        axis, me = (("dp_0", ix), ("dp_1", iy))[c]
        block = wg.at[pl.ds(1, 3), pl.ds(rows0, 48), pl.ds(*LANES[c])]
        return [remote(block, block, w1.at[0, i], w1.at[1, i], **{axis: turn(me, i)}) for i in (1, 2, 3)]

    def second(c, k):
        axis, me, line = (("dp_1", iy, iy), ("dp_0", ix, ix))[c]
        block = part(c, k, pl.multiple_of(192 * line, 192), 192)
        return [remote(block, block, w2.at[0, k, i], w2.at[1, k, i], **{axis: turn(me, i)}) for i in (1, 2, 3)]

    def third(c, k):
        block = part(c, k, 0, D)
        return remote(block, block, w3.at[0, k], w3.at[1, k], dp_2=1 - ic)

    def each_core(do):
        for c in (0, 1):
            @pl.when(ic == c)
            def _():
                do(c)

    ups = [
        remote(up.at[0, pl.ds(64, 16)], up.at[4 - i, pl.ds(64, 16)], usem.at[0, i], usem.at[1, 4 - i], heads=turn(iz, i))
        for i in (1, 2, 3)
    ]
    for c in ups:
        c.start()
    each_core(lambda c: [d.start() for d in over_z(c)])
    for c in late:
        c.start()
    each_core(lambda c: [d.wait_recv() for d in over_z(c)])
    each_core(lambda c: [d.start() for d in first(c)])
    spread(cot, ct, csem)
    each_core(lambda c: [d.wait_recv() for d in first(c)])
    each_core(lambda c: [d.start() for k in (1, 2, 3) for d in second(c, k)])
    for c in ups:
        c.wait_recv()

    row = jnp.where(mine == 0, kmask[0:1], jnp.where(mine == 1, kmask[1:2], kmask[2:3]))
    row = jnp.where(ic == 0, row, jnp.concatenate([row[:, 256:512], row[:, 0:256]], axis=1))
    row = jnp.where(row > 0, 0.0, -1e30).astype(F32)
    bias[...] = jnp.broadcast_to(row, (128, S)).T[:, 0:1]
    spread_wait(inputs, x, xsem)

    def fwd(k, _):
        @pl.when(k > 0)
        def _():
            def do(c):
                third(1 - c, k).wait_recv()
            each_core(do)

        @pl.when(owner)
        def _():
            project(k, x, wg, up, bias, knat, vnat, yt)

        @pl.when(k < 3)
        def _():
            def do(c):
                for d in second(c, k + 1):
                    d.wait_recv()
                third(c, k + 1).start()
            each_core(do)

        @pl.when(owner)
        def _():
            attend(k, knat, yt, sscr, p, rl, ctxt)

        return 0

    lax.fori_loop(0, G, fwd, 0)
    for c in late:
        c.wait()

    @pl.when(owner)
    def _():
        ctx = jnp.concatenate([ctxt[g].T for g in range(G)], axis=1)
        h1 = x[...].astype(F32) + nn(ctx, wo[...])
        xh, r = norm(h1)
        xhat1[...] = xh
        r1s[:, 0:1] = r
        n1v = xh * g1[...] + b1[...]
        n1b[...] = n1v.astype(BF)
        acc[...] = n1v

        def ffn(c, _):
            cols = pl.ds(pl.multiple_of(c * 2 * C, 2 * C), 2 * C)
            h = nn(n1b[...], wi[:, cols])
            a, da = gelu_pair(h)
            dact[:, cols] = da
            acc[...] += nn(a.astype(BF), wt[cols, :])
            return 0

        lax.fori_loop(0, FF // (2 * C), ffn, 0)
        xh2, r2 = norm(acc[...])
        act[...] = (xh2 * g2[...] + b2[...]).astype(BF)
        acc[...] = xh2
        r1s[:, 1:2] = r2

    def back(src, dst, sem):
        @pl.when(owner)
        def _():
            for t in range(4):
                @pl.when(rank != t)
                def _():
                    remote(src.at[pl.ds(t * Q, Q)], dst.at[mine], sem.at[0, t], sem.at[1, mine], heads=z_of(t)).start()

                @pl.when(rank == t)
                def _():
                    pltpu.make_async_copy(src.at[pl.ds(t * Q, Q)], dst.at[mine], sem.at[1, mine]).start()

    def back_end(src, dst, sem):
        for j in range(B):
            pltpu.make_async_copy(src.at[pl.ds(0, Q)], dst.at[j], sem.at[1, j]).wait()

        @pl.when(owner)
        def _():
            for t in range(4):
                @pl.when(rank != t)
                def _():
                    remote(src.at[pl.ds(t * Q, Q)], dst.at[mine], sem.at[0, t], sem.at[1, mine], heads=z_of(t)).wait_send()

    back(act, act_out, asem)
    spread_wait(cot, ct, csem)

    @pl.when(owner)
    def _():
        limit = lengths[mine]
        at = lax.broadcasted_iota(jnp.int32, (Q, 1), 0)
        valid = jnp.concatenate([at + z_of(t) * Q < limit for t in range(4)], axis=0)
        tangent = jnp.where(valid, ct[...].astype(F32), 0.0)
        gs = norm_back(tangent * g2[...], acc[...], r1s[:, 1:2])
        gnb[...] = gs.astype(BF)
        acc[...] = gs

        def ffn_back(c, _):
            cols = pl.ds(pl.multiple_of(c * 2 * C, 2 * C), 2 * C)
            ga = nt(gnb[...], wt[cols, :])
            gi = (ga * dact[:, cols]).astype(BF)
            acc[...] += nt(gi, wi[:, cols])
            return 0

        lax.fori_loop(0, FF // (2 * C), ffn_back, 0)
        gf1 = norm_back(acc[...] * g1[...], xhat1[...], r1s[:, 0:1])
        acc[...] = gf1
        gfb = gf1.astype(BF)
        for g in range(G):
            dot_ref[g] = nt(wo[192 * g : 192 * g + 192, :], gfb)

        def bwd(g, gm):
            attend_back(g, vnat, yt, p, rl, ctxt, dot_ref, dsscr, dyt)
            mid = yt[g, 576:592, :]
            first_rows = lax.broadcasted_iota(jnp.int32, (16, 192), 0) < 8
            gu = jnp.where(first_rows, nt(mid, dyt[g, 0:192, :]), nt(mid, dyt[g, 192:384, :]))
            msg[g, 0:16, 0:192] = gu * 2.0
            return gm + nn(up[g, 64:80, :], dyt[g, 0:384, :])

        gmb = lax.fori_loop(0, G, bwd, jnp.zeros((16, S), F32)).astype(BF)
        gd = nn(gmb, x[...])
        for q in range(4):
            gdp[q, :, 0:192] = gd[:, 192 * q : 192 * q + 192]
        for k in range(G):
            msg[k, 16:32, 0:192] = gdp[turn(iz, k), :, 0:192]
            dyt[k, 576:GW, :] = jnp.concatenate(
                [gmb if k == 0 else jnp.zeros((16, S), BF), jnp.zeros((48, S), BF)], axis=0
            )

    zsum = [remote(msg.at[i], redz.at[4 - i], gz.at[0, i], gz.at[1, 4 - i], heads=turn(iz, i)) for i in (1, 2, 3)]

    @pl.when(owner)
    def _():
        for c in zsum:
            c.start()

    @pl.when(owner)
    def _():
        total = acc[...]
        for g in range(G):
            total = total + nt(dyt[g].T, wg[g])
        igb[...] = total.astype(BF)

    back(igb, ig_out, isem)

    @pl.when(owner)
    def _():
        redz[0] = msg[0]

    @pl.when(rank == 3)
    def _():
        redz[0] = jnp.zeros((32, 256), F32)

    for i in (1, 2, 3):
        from_owner = turn(rank, i) != 3

        @pl.when(from_owner)
        def _():
            pltpu.make_async_copy(msg.at[i], redz.at[i], gz.at[1, i]).wait()
            redz[0] += redz[i]

    step = remote(redz.at[0], redc, gc.at[0], gc.at[1], dp_2=1 - ic)
    step.start()
    step.wait()

    def line(value, buf, sem, axis, me):
        buf[me] = value
        copies = [remote(buf.at[me], buf.at[me], sem.at[0, i], sem.at[1, i], **{axis: turn(me, i)}) for i in (1, 2, 3)]
        for c in copies:
            c.start()
        for c in copies:
            c.wait()
        return buf[0] + buf[1] + buf[2] + buf[3]

    total = line(redz[0] + redc[...], redx, gx, "dp_0", ix)
    total = line(total, redy, gy, "dp_1", iy)
    gu_out[...] = total[0:16]
    gd_out[iz] = total[16:32]
    copies = [
        remote(gd_out.at[iz], gd_out.at[iz], gf.at[0, i], gf.at[1, i], heads=turn(iz, i)) for i in (1, 2, 3)
    ]
    for c in copies:
        c.start()
    for c in copies:
        c.wait()

    back_end(act, act_out, asem)
    back_end(igb, ig_out, isem)
    spread_end(inputs, x, xsem)
    spread_end(cot, ct, csem)
    for c in ups:
        c.wait_send()
    each_core(lambda c: [d.wait_send() for d in over_z(c) + first(c)])
    each_core(lambda c: [d.wait_send() for k in (1, 2, 3) for d in second(c, k) + [third(c, k)]])

    @pl.when(owner)
    def _():
        for c in zsum:
            c.wait_send()


def finish(act_in, ig_in, gd, gu, act, ig, gdq, guq, gdv, guv):
    act[...] = act_in[...]
    ig[...] = ig_in[...].astype(F32)

    @pl.when(pl.program_id(0) == 0)
    def _():
        cols = jnp.concatenate([gd[q, :, 0:192] for q in range(4)], axis=1).T
        gdq[...] = cols[:, 0:8]
        gdv[...] = cols[:, 8:16]
        guq[...] = gu[0:8, 0:192]
        guv[...] = gu[8:16, 0:192]


def scratch():
    V, dma = pltpu.VMEM, pltpu.SemaphoreType.DMA
    return [
        V((S, D), BF), V((S, D), BF), V((D, 192), BF), V((D, 192), BF), V((D, 192), BF),
        V((D, D), BF), V((D, FF), BF), V((FF, D), BF), V((G, D, GW), BF), V((G, 128, 384), BF),
        V((S, D), BF), V((S, D), BF),
        V((S, 1), F32), V((G, S, 256), BF), V((G, S, 256), BF), V((G, GW, S), BF),
        V((3, 2, S, 256), F32), V((12, S, S), BF), V((12, 1, S), F32), V((G, 192, S), BF),
        V((S, D), F32), V((S, 2), F32), V((S, D), BF),
        V((S, FF), F32), V((S, D), F32), V((G, 192, S), F32), V((3, S, S), BF), V((G, GW, S), BF), V((S, D), BF),
        V((4, 32, 256), F32), V((4, 32, 256), F32), V((32, 256), F32), V((4, 32, 256), F32), V((4, 32, 256), F32),
        V((4, 16, 256), F32),
        dma((9,)), dma((2, 4)), dma((2, 4)), dma((2, 4)), dma((2, 4)), dma((2, 4)), dma((2, 4, 4)), dma((2, 4)),
        dma((2, 4)), dma((2, 4)), dma((2, 4)), dma((2,)), dma((2, 4)), dma((2, 4)), dma((2, 4)),
    ]


def per_device(inputs, key_mask, lengths, cotangent, wq, wk, wv, w_out, w_inner, w_outer, g1, b1, g2, b2, dq, uq, dv, uv):
    vm, hbm = pl.BlockSpec(memory_space=pltpu.VMEM), pl.BlockSpec(memory_space=pl.ANY)
    shape = jax.ShapeDtypeStruct
    act, ig, gd, gu = pl.pallas_call(
        layer,
        out_shape=(shape((B, Q, D), BF), shape((B, Q, D), BF), shape((4, 16, 256), F32), shape((16, 256), F32)),
        in_specs=[hbm, hbm, vm, pl.BlockSpec(memory_space=pltpu.SMEM)] + [hbm] * 6 + [vm] * 8,
        out_specs=(hbm, hbm, vm, vm),
        scratch_shapes=scratch(),
        compiler_params=pltpu.CompilerParams(
            collective_id=0, has_side_effects=True, vmem_limit_bytes=62 * 2**20
        ),
    )(
        inputs, cotangent, key_mask, lengths, wq, wk, wv, w_out, w_inner, w_outer,
        g1[None], b1[None], g2[None], b2[None], dq, uq, dv, uv,
    )
    one = pl.BlockSpec((1, Q, D), lambda j: (j, 0, 0))

    def whole(*dims):
        return pl.BlockSpec(dims, lambda j: (0,) * len(dims))

    act, ig, gdq, guq, gdv, guv = pl.pallas_call(
        finish,
        grid=(B,),
        out_shape=(
            shape((B, Q, D), BF), shape((B, Q, D), F32),
            shape((D, 8), F32), shape((8, 192), F32), shape((D, 8), F32), shape((8, 192), F32),
        ),
        in_specs=[one, one, whole(4, 16, 256), whole(16, 256)],
        out_specs=(one, one, whole(D, 8), whole(8, 192), whole(D, 8), whole(8, 192)),
    )(act, ig, gd, gu)
    return act, ig, gdq, guq, gdv, guv


def solution(mesh):
    finer = Mesh(
        mesh.devices.reshape(4, 4, 2, mesh.shape["heads"]), ("dp_0", "dp_1", "dp_2", "heads")
    )
    rows, cols, same = P(DP, "heads", None), P(None, "heads"), P()
    return jax.shard_map(
        per_device,
        mesh=finer,
        in_specs=(rows, P(DP, None), P(DP), rows, cols, cols, cols) + (same,) * 8 + (cols, same, cols),
        out_specs=(rows, rows, same, cols, same, cols),
        check_vma=False,
    )
```

```python
import functools

import jax
import jax.numpy as jnp
from jax import lax
from jax.experimental import pallas as pl
from jax.experimental.pallas import tpu as pltpu
from jax.sharding import Mesh
from jax.sharding import PartitionSpec as P

BF, F32 = jnp.bfloat16, jnp.float32
S, D, FF, HD, G = 512, 768, 3072, 64, 4
B, Q = 3, 128
GW = 640
C = 512
NT = (((1,), (1,)), ((), ()))
DP = ("dp_0", "dp_1", "dp_2")
MESH = pl.DeviceIdType.MESH


def nn(a, b):
    return jnp.dot(a, b, preferred_element_type=F32)


def nt(a, b):
    return lax.dot_general(a, b, NT, preferred_element_type=F32)


def middle(x, down, mid):
    mid[0:16, :] = nt(down[...], x[...]).astype(BF)
    mid[16:64, :] = jnp.zeros((48, S), BF)


def project(g, x, wg, up, mid, bias, knat, vnat, yt):
    xv = x[...]
    at = pl.multiple_of(g * 576, 576)
    upt = jnp.concatenate([up[g], jnp.zeros((112, 384), BF)], axis=0).T
    middle_rows = jnp.concatenate([mid[...], jnp.zeros((64, S), BF)], axis=0)
    kt = jnp.concatenate([nt(wg[pl.ds(at + 384, 192), :], xv).astype(BF), bias[...]], axis=0)
    yt[g, 384:GW, :] = kt
    knat[g] = kt.T
    qv = nt(wg[pl.ds(at, 384), :], xv) + nn(upt, middle_rows)
    vt = qv[192:384].astype(BF)
    yt[g, 0:192, :] = (qv[0:192].astype(BF).astype(F32) * 0.125).astype(BF)
    yt[g, 192:384, :] = vt
    vnat[g] = jnp.concatenate([jnp.zeros((64, S), BF), vt], axis=0).T


def pad_rows(piece, before, total):
    parts = []
    if before:
        parts.append(jnp.zeros((before, S), BF))
    parts.append(piece)
    after = total - before - piece.shape[0]
    if after:
        parts.append(jnp.zeros((after, S), BF))
    return jnp.concatenate(parts, axis=0)


def attend(g, knat, yt, sscr, p, rl, ctxt):
    one_row = (lax.broadcasted_iota(jnp.int32, (64, S), 0) == 63).astype(BF)
    ones = jnp.ones((16, S), BF)
    kb = knat[g]
    for j in range(3):
        rhs = jnp.concatenate([pad_rows(yt[g, 64 * j : 64 * j + 64, :], 64 * j, 192), one_row], axis=0)
        for half in range(2):
            cols = slice(256 * half, 256 * half + 256)
            s = nn(kb, rhs[:, cols])
            sscr[j, half] = s
            m = jnp.max(s, axis=0, keepdims=True)
            p[g * 3 + j, :, cols] = jnp.exp(sscr[j, half] - m).astype(BF)
        vt = jnp.concatenate([yt[g, 192 + 64 * j : 256 + 64 * j, :], ones], axis=0)
        ot = nn(vt, p[g * 3 + j])
        rinv = 1.0 / ot[64:65]
        rl[g * 3 + j] = rinv
        ctxt[g, 64 * j : 64 * j + 64, :] = (ot[0:64] * rinv).astype(BF)


def attend_back(g, vnat, yt, p, rl, ctxt, dot_ref, dsscr, dyt):
    vb = vnat[g]
    at = pl.multiple_of(g * 576, 576)
    for j in range(3):
        h = g * 3 + j
        rows = slice(64 * j, 64 * j + 64)
        do = (dot_ref[g, rows, :] * rl[h]).astype(BF)
        dsum = jnp.sum(do.astype(F32) * ctxt[g, rows, :].astype(F32), axis=0, keepdims=True)
        rhs = pad_rows(do, 64 + 64 * j, 256)
        for half in range(2):
            cols = slice(256 * half, 256 * half + 256)
            dp = nn(vb, rhs[:, cols])
            dsscr[j, :, cols] = (p[h, :, cols].astype(F32) * (dp - dsum[:, cols])).astype(BF)
        dyt[pl.ds(at + 192 + 64 * j, 64), :] = nt(do, p[h]).astype(BF)
        ds = dsscr[j]
        dyt[pl.ds(at + 384 + 64 * j, 64), :] = nt(yt[g, rows, :], ds).astype(BF)
        dyt[pl.ds(at + 64 * j, 64), :] = (nn(yt[g, 384 + 64 * j : 448 + 64 * j, :], ds) * 0.125).astype(BF)


def gelu_pair(v):
    e = jnp.exp(v * v * -0.5)
    t = 1.0 / (1.0 + 0.23164189 * jnp.abs(v))
    tail = t * (0.127414796 + t * (-0.142248368 + t * (0.7107068705 + t * (-0.7265760135 + t * 0.5307027145)))) * e
    cdf = jnp.where(v >= 0.0, 1.0 - tail, tail)
    return v * cdf, cdf + v * (e * 0.3989422804)


def norm(h):
    mean = jnp.mean(h, axis=-1, keepdims=True)
    c = h - mean
    r = lax.rsqrt(jnp.mean(c * c, axis=-1, keepdims=True) + 1e-5)
    return c * r, r


def norm_back(n, xhat, r):
    return r * (n - jnp.mean(n, axis=-1, keepdims=True) - xhat * jnp.mean(n * xhat, axis=-1, keepdims=True))


def chunk(c):
    return pl.ds(pl.multiple_of(c * C, C), C)


def feed_forward(n1b, wi, wt, ha, hb, aa, ab, dact, acc):
    last = FF // C - 1

    def act(h, a, c):
        v, d = gelu_pair(h[...])
        a[...] = v.astype(BF)
        dact[:, chunk(c)] = d.astype(dact.dtype)

    ha[...] = nn(n1b[...], wi[:, chunk(0)])

    def pair(i, _):
        c = 2 * i
        hb[...] = nn(n1b[...], wi[:, chunk(c + 1)])
        act(ha, aa, c)
        ha[...] = nn(n1b[...], wi[:, chunk(jnp.minimum(c + 2, last))])
        acc[...] += nn(aa[...], wt[chunk(c), :])
        act(hb, ab, c + 1)
        acc[...] += nn(ab[...], wt[chunk(c + 1), :])
        return 0

    lax.fori_loop(0, FF // C // 2, pair, 0)


def feed_back(gnb, wi, wt, ga, aa, ab, dact, acc):
    last = FF // C - 1

    def grad(c):
        return nt(gnb[...], wt[chunk(c), :])

    def through(h, a, c):
        a[...] = (h * dact[:, chunk(c)].astype(F32)).astype(BF)

    through(grad(0), aa, 0)

    def pair(i, _):
        c = 2 * i
        through(grad(c + 1), ab, c + 1)
        acc[...] += nt(aa[...], wi[:, chunk(c)])
        n = jnp.minimum(c + 2, last)
        through(grad(n), aa, n)
        acc[...] += nt(ab[...], wi[:, chunk(c + 1)])
        return 0

    lax.fori_loop(0, FF // C // 2, pair, 0)
def remote(src, dst, send, recv, **where):
    return pltpu.make_async_remote_copy(
        src_ref=src, dst_ref=dst, send_sem=send, recv_sem=recv, device_id=where, device_id_type=MESH
    )


def layer(
    inputs, cot, kmask, lengths, wq, wk, wv, w_out, w_inner, w_outer, g1, b1, g2, b2, dq, uq, dv, uv,
    act_out, ig_out, gd_out, gu_out,
    x, ct, wo, wi, wt, wg, up, down, act, igb,
    bias, mid, knat, vnat, yt, sscr, p, rl, ctxt, xhat1, r1s, n1b, ha, hb, aa, ab, dact, acc, dot_ref, dsscr, dyt, gnb,
    msg, redz, redc, redx, redy, gdp, gmid,
    lsem, xsem, csem, wsem, usem, w1, w2, w3, asem, isem, gz, gc, gx, gy, gf,
):
    ix, iy, ic, iz = (lax.axis_index(a) for a in ("dp_0", "dp_1", "dp_2", "heads"))
    rank = lax.rem(iz + 2 * ic, 4)
    owner = rank < 3
    mine = jnp.minimum(rank, 2)

    def z_of(r):
        return lax.rem(r + 2 * ic, 4)

    def turn(i, by):
        return lax.rem(i + by, 4)

    loads = [
        pltpu.make_async_copy(w, wg.at[pl.ds(192 * n, 192)], lsem.at[n]) for n, w in enumerate((wq, wv, wk))
    ]
    for c in loads:
        c.start()
    late = [pltpu.make_async_copy(w_inner, wi, lsem.at[3]), pltpu.make_async_copy(w_outer, wt, lsem.at[4])]
    for k in range(G):
        at = pl.multiple_of(turn(iz, k) * 192, 192)
        late.append(pltpu.make_async_copy(w_out.at[pl.ds(at, 192)], wo.at[pl.ds(192 * k, 192)], lsem.at[5 + k]))

    barrier = pltpu.get_barrier_semaphore()
    peers = [{"dp_2": 1 - ic}]
    for i in (1, 2, 3):
        peers += [{"heads": turn(iz, i)}, {"dp_0": turn(ix, i)}, {"dp_1": turn(iy, i)}]
    for where in peers:
        pl.semaphore_signal(barrier, inc=1, device_id=where, device_id_type=MESH)
    pl.semaphore_wait(barrier, 10)

    def slot(ref, r):
        return ref.at[pl.ds(pl.multiple_of(r * Q, Q), Q)]

    def spread(src, dst, sem):
        for j in range(B):
            @pl.when(rank != j)
            def _():
                remote(src.at[j], slot(dst, rank), sem.at[0, j], sem.at[1, rank], heads=z_of(j)).start()

            @pl.when(rank == j)
            def _():
                pltpu.make_async_copy(src.at[j], slot(dst, rank), sem.at[1, j]).start()

    def spread_wait(src, dst, sem):
        @pl.when(owner)
        def _():
            for r in range(4):
                pltpu.make_async_copy(src.at[0], dst.at[pl.ds(r * Q, Q)], sem.at[1, r]).wait()

    def spread_end(src, dst, sem):
        for j in range(B):
            @pl.when(rank != j)
            def _():
                remote(src.at[j], slot(dst, rank), sem.at[0, j], sem.at[1, rank], heads=z_of(j)).wait_send()

    spread(inputs, x, xsem)

    for c in loads:
        c.wait()
    down[...] = jnp.concatenate([dq[...].astype(F32), dv[...].astype(F32)], axis=0).astype(BF)
    zero8 = jnp.zeros((8, 192), F32)
    both = jnp.concatenate(
        [
            jnp.concatenate([uq[...].astype(F32), zero8], axis=1),
            jnp.concatenate([zero8, uv[...].astype(F32)], axis=1),
        ],
        axis=0,
    )
    up[0] = (2.0 * both).astype(BF)
    row_of = ((iy, ix), (ix, iy))

    def part(c, k, at, count):
        return wg.at[pl.ds(pl.multiple_of(576 * k + at, 16), count), pl.ds(384 * c, 384)]

    def over_z(c):
        b, a = row_of[c]
        return [
            remote(part(c, 0, 192 * b + 48 * a, 48), part(c, 4 - i, 192 * b + 48 * a, 48), wsem.at[0, i],
                   wsem.at[1, 4 - i], heads=turn(iz, i))
            for i in (1, 2, 3)
        ]

    def first(c):
        b, a = row_of[c]
        axis = ("dp_0", "dp_1")[c]
        blocks = [part(c, k, 192 * b + 48 * a, 48) for k in (0, 1, 2, 3)]
        return [
            remote(blocks[k], blocks[k], w1.at[0, k, i], w1.at[1, k, i], **{axis: turn(a, i)})
            for k in (1, 2, 3) for i in (1, 2, 3)
        ]

    def second(c, k, i, back):
        b, a = row_of[c]
        axis = ("dp_1", "dp_0")[c]
        block = part(c, k, 192 * (turn(b, 4 - i) if back else b), 192)
        return remote(block, block, w2.at[0, k, i], w2.at[1, k, i], **{axis: turn(b, i)})

    def holds(c):
        return row_of[c][0] < 3

    def second_start(c, k):
        for i in (1, 2, 3):
            second(c, k, i, False).start()

    def second_recv(c, k):
        for i in (1, 2, 3):
            @pl.when(turn(row_of[c][0], 4 - i) < 3)
            def _():
                second(c, k, i, True).wait_recv()

    def third(c, k):
        block = part(c, k, 0, 576)
        return remote(block, block, w3.at[0, k], w3.at[1, k], dp_2=1 - ic)

    def each_core(do, only=lambda c: True):
        for c in (0, 1):
            @pl.when(jnp.logical_and(ic == c, only(c)))
            def _():
                do(c)

    ups = [
        remote(up.at[0], up.at[4 - i], usem.at[0, i], usem.at[1, 4 - i], heads=turn(iz, i))
        for i in (1, 2, 3)
    ]
    for c in ups:
        c.start()
    each_core(lambda c: [d.start() for d in over_z(c)], holds)
    for c in late:
        c.start()
    each_core(lambda c: [d.wait_recv() for d in over_z(c)], holds)
    each_core(lambda c: [d.start() for d in first(c)], holds)
    spread(cot, ct, csem)
    for k in (1, 2, 3):
        each_core(lambda c: [d.wait_recv() for d in first(c)[3 * k - 3 : 3 * k]], holds)
        each_core(lambda c: second_start(c, k), holds)
    for c in ups:
        c.wait_recv()

    row = jnp.where(mine == 0, kmask[0:1], jnp.where(mine == 1, kmask[1:2], kmask[2:3]))
    row = jnp.where(ic == 0, row, jnp.concatenate([row[:, 256:512], row[:, 0:256]], axis=1))
    row = jnp.where(row > 0, 0.0, -1e30).astype(F32)
    bias[...] = jnp.where(lax.broadcasted_iota(jnp.int32, (64, S), 0) == 63, row, 0.0).astype(BF)
    spread_wait(inputs, x, xsem)
    pl.when(owner)(lambda: middle(x, down, mid))

    def fwd(k, _):
        @pl.when(k > 0)
        def _():
            def do(c):
                third(1 - c, k).wait_recv()
            each_core(do)

        @pl.when(owner)
        def _():
            project(k, x, wg, up, mid, bias, knat, vnat, yt)

        @pl.when(k < 3)
        def _():
            def do(c):
                second_recv(c, k + 1)
                third(c, k + 1).start()
            each_core(do)

        @pl.when(owner)
        def _():
            attend(k, knat, yt, sscr, p, rl, ctxt)

        return 0

    lax.fori_loop(0, G, fwd, 0)
    for c in late:
        c.wait()

    @pl.when(owner)
    def _():
        ctx = jnp.concatenate([ctxt[g].T for g in range(G)], axis=1)
        h1 = x[...].astype(F32) + nn(ctx, wo[...])
        xh, r = norm(h1)
        xhat1[...] = xh
        r1s[:, 0:1] = r
        n1v = xh * g1[...][None] + b1[...][None]
        n1b[...] = n1v.astype(BF)
        acc[...] = n1v

        feed_forward(n1b, wi, wt, ha, hb, aa, ab, dact, acc)
        xh2, r2 = norm(acc[...])
        act[...] = (xh2 * g2[...][None] + b2[...][None]).astype(BF)
        acc[...] = xh2
        r1s[:, 1:2] = r2

    def back(src, dst, sem):
        @pl.when(owner)
        def _():
            for t in range(4):
                @pl.when(rank != t)
                def _():
                    remote(src.at[pl.ds(t * Q, Q)], dst.at[mine], sem.at[0, t], sem.at[1, mine], heads=z_of(t)).start()

                @pl.when(rank == t)
                def _():
                    pltpu.make_async_copy(src.at[pl.ds(t * Q, Q)], dst.at[mine], sem.at[1, mine]).start()

    def back_end(src, dst, sem):
        for j in range(B):
            pltpu.make_async_copy(src.at[pl.ds(0, Q)], dst.at[j], sem.at[1, j]).wait()

        @pl.when(owner)
        def _():
            for t in range(4):
                @pl.when(rank != t)
                def _():
                    remote(src.at[pl.ds(t * Q, Q)], dst.at[mine], sem.at[0, t], sem.at[1, mine], heads=z_of(t)).wait_send()

    back(act, act_out, asem)
    spread_wait(cot, ct, csem)

    @pl.when(owner)
    def _():
        limit = lengths[mine]
        at = lax.broadcasted_iota(jnp.int32, (Q, 1), 0)
        valid = jnp.concatenate([at + z_of(t) * Q < limit for t in range(4)], axis=0)
        tangent = jnp.where(valid, ct[...].astype(F32), 0.0)
        gs = norm_back(tangent * g2[...][None], acc[...], r1s[:, 1:2])
        gnb[...] = gs.astype(BF)
        acc[...] = gs

        feed_back(gnb, wi, wt, ha, aa, ab, dact, acc)
        gf1 = norm_back(acc[...] * g1[...][None], xhat1[...], r1s[:, 0:1])
        acc[...] = gf1
        gfb = gf1.astype(BF)
        for g in range(G):
            dot_ref[g] = nt(wo[192 * g : 192 * g + 192, :], gfb)

        def bwd(g, gm):
            attend_back(g, vnat, yt, p, rl, ctxt, dot_ref, dsscr, dyt)
            at = pl.multiple_of(g * 576, 576)
            first_rows = lax.broadcasted_iota(jnp.int32, (16, 192), 0) < 8
            gu = nt(mid[0:16, :], dyt[pl.ds(at, 384), :])
            msg[g, 0:16, 0:192] = jnp.where(first_rows, gu[:, 0:192], gu[:, 192:384]) * 2.0
            return gm + nn(up[g], dyt[pl.ds(at, 384), :])

        gmb = lax.fori_loop(0, G, bwd, jnp.zeros((16, S), F32)).astype(BF)
        gd = nn(gmb, x[...])
        for q in range(4):
            gdp[q, :, 0:192] = gd[:, 192 * q : 192 * q + 192]
        for k in range(G):
            msg[k, 16:32, 0:192] = gdp[turn(iz, k), :, 0:192]
        gmid[...] = gmb

    zsum = [remote(msg.at[i], redz.at[4 - i], gz.at[0, i], gz.at[1, 4 - i], heads=turn(iz, i)) for i in (1, 2, 3)]

    @pl.when(owner)
    def _():
        for c in zsum:
            c.start()

    @pl.when(owner)
    def _():
        gmt = jnp.concatenate([gmid[...], jnp.zeros((112, S), BF)], axis=0).T
        dn = jnp.concatenate([down[...], jnp.zeros((112, D), BF)], axis=0)
        total = acc[...] + nn(dyt[...].T, wg[...]) + nn(gmt, dn)
        igb[...] = total.astype(BF)

    back(igb, ig_out, isem)

    @pl.when(owner)
    def _():
        redz[0] = msg[0]

    @pl.when(rank == 3)
    def _():
        redz[0] = jnp.zeros((32, 256), F32)

    for i in (1, 2, 3):
        from_owner = turn(rank, i) != 3

        @pl.when(from_owner)
        def _():
            pltpu.make_async_copy(msg.at[i], redz.at[i], gz.at[1, i]).wait()
            redz[0] += redz[i]

    step = remote(redz.at[0], redc, gc.at[0], gc.at[1], dp_2=1 - ic)
    step.start()
    step.wait()

    def line(value, buf, sem, axis, me):
        buf[me] = value
        copies = [remote(buf.at[me], buf.at[me], sem.at[0, i], sem.at[1, i], **{axis: turn(me, i)}) for i in (1, 2, 3)]
        for c in copies:
            c.start()
        for c in copies:
            c.wait()
        return buf[0] + buf[1] + buf[2] + buf[3]

    total = line(redz[0] + redc[...], redx, gx, "dp_0", ix)
    total = line(total, redy, gy, "dp_1", iy)
    gu_out[...] = total[0:16]
    gd_out[iz] = total[16:32]
    copies = [
        remote(gd_out.at[iz], gd_out.at[iz], gf.at[0, i], gf.at[1, i], heads=turn(iz, i)) for i in (1, 2, 3)
    ]
    for c in copies:
        c.start()
    for c in copies:
        c.wait()

    back_end(act, act_out, asem)
    back_end(igb, ig_out, isem)
    spread_end(inputs, x, xsem)
    spread_end(cot, ct, csem)
    for c in ups:
        c.wait_send()
    each_core(lambda c: [d.wait_send() for d in over_z(c) + first(c)], holds)
    each_core(lambda c: [second(c, k, i, False).wait_send() for k in (1, 2, 3) for i in (1, 2, 3)], holds)
    each_core(lambda c: [third(c, k).wait_send() for k in (1, 2, 3)])

    @pl.when(owner)
    def _():
        for c in zsum:
            c.wait_send()


def finish(act_in, ig_in, gd, gu, act, ig, gdq, guq, gdv, guv):
    act[...] = act_in[...]
    ig[...] = ig_in[...].astype(F32)
    down = jnp.concatenate([gd[q, :, 0:192] for q in range(4)], axis=1)
    gdq[...] = down[0:8]
    gdv[...] = down[8:16]
    guq[...] = gu[0:8, 0:192]
    guv[...] = gu[8:16, 0:192]


def scratch():
    V, dma = pltpu.VMEM, pltpu.SemaphoreType.DMA
    return [
        V((S, D), BF), V((S, D), BF), V((D, D), BF), V((D, FF), BF), V((FF, D), BF), V((G * 576, D), BF),
        V((G, 16, 384), BF), V((16, D), BF), V((S, D), BF), V((S, D), BF),
        V((64, S), BF), V((64, S), BF), V((G, S, 256), BF), V((G, S, 256), BF), V((G, GW, S), BF),
        V((3, 2, S, 256), F32), V((12, S, S), BF), V((12, 1, S), F32), V((G, 192, S), BF),
        V((S, D), F32), V((S, 2), F32), V((S, D), BF),
        V((S, C), F32), V((S, C), F32), V((S, C), BF), V((S, C), BF), V((S, FF), F32), V((S, D), F32),
        V((G, 192, S), F32), V((3, S, S), BF), V((G * 576, S), BF), V((S, D), BF),
        V((4, 32, 256), F32), V((4, 32, 256), F32), V((32, 256), F32), V((4, 32, 256), F32), V((4, 32, 256), F32),
        V((4, 16, 256), F32), V((16, S), BF),
        dma((9,)), dma((2, 4)), dma((2, 4)), dma((2, 4)), dma((2, 4)), dma((2, 4, 4)), dma((2, 4, 4)), dma((2, 4)),
        dma((2, 4)), dma((2, 4)), dma((2, 4)), dma((2,)), dma((2, 4)), dma((2, 4)), dma((2, 4)),
    ]


def per_device(inputs, key_mask, lengths, cotangent, wq, wk, wv, w_out, w_inner, w_outer, g1, b1, g2, b2, dq, uq, dv, uv):
    vm, hbm = pl.BlockSpec(memory_space=pltpu.VMEM), pl.BlockSpec(memory_space=pl.ANY)
    shape = jax.ShapeDtypeStruct
    act, ig, gd, gu = pl.pallas_call(
        layer,
        out_shape=(shape((B, Q, D), BF), shape((B, Q, D), BF), shape((4, 16, 256), F32), shape((16, 256), F32)),
        in_specs=[hbm, hbm, vm, pl.BlockSpec(memory_space=pltpu.SMEM)] + [hbm] * 6 + [vm] * 8,
        out_specs=(hbm, hbm, vm, vm),
        scratch_shapes=scratch(),
        compiler_params=pltpu.CompilerParams(
            collective_id=0, has_side_effects=True, vmem_limit_bytes=62 * 2**20
        ),
    )(
        inputs, cotangent, key_mask, lengths, wq.T, wk.T, wv.T, w_out, w_inner, w_outer,
        g1, b1, g2, b2, dq.T, uq, dv.T, uv,
    )
    act, ig, gdq, guq, gdv, guv = pl.pallas_call(
        finish,
        out_shape=(
            shape((B, Q, D), BF), shape((B, Q, D), F32),
            shape((8, D), F32), shape((8, 192), F32), shape((8, D), F32), shape((8, 192), F32),
        ),
        in_specs=[vm] * 4,
        out_specs=(vm,) * 6,
    )(act, ig, gd, gu)
    return act, ig, gdq.T, guq, gdv.T, guv


def solution(mesh):
    finer = Mesh(
        mesh.devices.reshape(4, 4, 2, mesh.shape["heads"]), ("dp_0", "dp_1", "dp_2", "heads")
    )
    rows, cols, same = P(DP, "heads", None), P(None, "heads"), P()
    return jax.shard_map(
        per_device,
        mesh=finer,
        in_specs=(rows, P(DP, None), P(DP), rows, cols, cols, cols) + (same,) * 8 + (cols, same, cols),
        out_specs=(rows, rows, same, cols, same, cols),
        check_vma=False,
    )
```

```python
import functools

import jax
import jax.numpy as jnp
from jax import lax
from jax.experimental import pallas as pl
from jax.experimental.pallas import tpu as pltpu
from jax.sharding import Mesh
from jax.sharding import PartitionSpec as P

BF, F32 = jnp.bfloat16, jnp.float32
S, D, FF, HD, G = 512, 768, 3072, 64, 4
B, Q = 3, 128
GW = 640
C = 512
NT = (((1,), (1,)), ((), ()))
DP = ("dp_0", "dp_1", "dp_2")
MESH = pl.DeviceIdType.MESH


def nn(a, b):
    return jnp.dot(a, b, preferred_element_type=F32)


def nt(a, b):
    return lax.dot_general(a, b, NT, preferred_element_type=F32)


def middle(x, wg, mid):
    mid[0:16, :] = nt(wg[576:592, :], x[...]).astype(BF)
    mid[16:64, :] = jnp.zeros((48, S), BF)


def project(g, x, wg, up, mid, bias, knat, vnat, yt):
    y = nt(wg[GW * g : GW * g + 576, :], x[...])
    upt = jnp.concatenate([up[g], jnp.zeros((112, 384), BF)], axis=0).T
    qv = y[0:384] + nn(upt[:, 0:64], mid[...])
    vt = qv[192:384].astype(BF)
    yt[g, 0:192, :] = (qv[0:192].astype(BF).astype(F32) * 0.125).astype(BF)
    yt[g, 192:384, :] = vt
    vnat[g] = jnp.concatenate([jnp.zeros((64, S), BF), vt], axis=0).T
    kt = jnp.concatenate([y[384:576].astype(BF), bias[...]], axis=0)
    yt[g, 384:GW, :] = kt
    knat[g] = kt.T


def pad_rows(piece, before, total):
    parts, lanes = [], piece.shape[1]
    if before:
        parts.append(jnp.zeros((before, lanes), BF))
    parts.append(piece)
    after = total - before - piece.shape[0]
    if after:
        parts.append(jnp.zeros((after, lanes), BF))
    return jnp.concatenate(parts, axis=0)


def staged(units, *stages):
    for step in range(len(units) + len(stages) - 1):
        for n, stage in enumerate(stages):
            if 0 <= step - n < len(units):
                stage(step - n, *units[step - n])


def half_cols(half):
    return slice(256 * half, 256 * half + 256)


def attend(units, place, knat, yt, sscr, p, rl, ctxt):
    maxima = {}

    def scores(u, g, j, half):
        cols = half_cols(half)
        last = (lax.broadcasted_iota(jnp.int32, (64, 256), 0) == 63).astype(BF)
        rhs = jnp.concatenate([pad_rows(yt[g, 64 * j : 64 * j + 64, cols], 64 * j, 192), last], axis=0)
        s = nn(knat[g], rhs)
        sscr[u % 3] = s
        maxima[u] = jnp.max(s, axis=0, keepdims=True)

    def weights(u, g, j, half):
        p[g * 3 + j, :, half_cols(half)] = jnp.exp(sscr[u % 3] - maxima[u]).astype(BF)

    def mix(u, g, j, half):
        cols = half_cols(half)
        vt = jnp.concatenate([yt[g, 192 + 64 * j : 256 + 64 * j, :], jnp.ones((16, S), BF)], axis=0)
        ot = nn(vt, p[g * 3 + j, :, cols])
        rinv = 1.0 / ot[64:65]
        rl[g * 3 + j, :, cols] = rinv
        ctxt[place(g), 64 * j : 64 * j + 64, cols] = (ot[0:64] * rinv).astype(BF)

    staged(units, scores, weights, mix)


def attend_back(units, place, vnat, yt, p, rl, ctxt, dot_ref, dosc, dsscr, dkv, dyt):
    def grads(u, g, j, half):
        rows, cols = slice(64 * j, 64 * j + 64), half_cols(half)
        do = (dot_ref[place(g), rows, cols].astype(F32) * rl[g * 3 + j, :, cols]).astype(BF)
        dosc[u % 3] = do
        dsum = jnp.sum(do.astype(F32) * ctxt[place(g), rows, cols].astype(F32), axis=0, keepdims=True)
        dp = nn(vnat[g], pad_rows(do, 64 + 64 * j, 256))
        dsscr[u % 3] = (p[g * 3 + j, :, cols].astype(F32) * (dp - dsum)).astype(BF)

    def products(u, g, j, half):
        h, cols, at = g * 3 + j, half_cols(half), GW * g + 64 * j
        ds = dsscr[u % 3]
        dv = nt(dosc[u % 3], p[h, :, cols])
        dk = nt(yt[g, 64 * j : 64 * j + 64, cols], ds)
        dyt[at : at + 64, cols] = (nn(yt[g, 384 + 64 * j : 448 + 64 * j, :], ds) * 0.125).astype(BF)
        if half == 0:
            dkv[h, 0], dkv[h, 1] = dv, dk
        else:
            dyt[at + 192 : at + 256, :] = (dkv[h, 0] + dv).astype(BF)
            dyt[at + 384 : at + 448, :] = (dkv[h, 1] + dk).astype(BF)

    staged(units, grads, products)


def gelu_pair(v):
    e = jnp.exp(v * v * -0.5)
    t = 1.0 / (1.0 + 0.23164189 * jnp.abs(v))
    tail = t * (0.127414796 + t * (-0.142248368 + t * (0.7107068705 + t * (-0.7265760135 + t * 0.5307027145)))) * e
    cdf = jnp.where(v >= 0.0, 1.0 - tail, tail)
    return v * cdf, cdf + v * (e * 0.3989422804)


def norm(h):
    mean = jnp.mean(h, axis=-1, keepdims=True)
    c = h - mean
    r = lax.rsqrt(jnp.mean(c * c, axis=-1, keepdims=True) + 1e-5)
    return c * r, r


def norm_back(n, xhat, r):
    return r * (n - jnp.mean(n, axis=-1, keepdims=True) - xhat * jnp.mean(n * xhat, axis=-1, keepdims=True))


def chunk(c):
    return pl.ds(pl.multiple_of(c * C, C), C)


def feed_forward(n1b, wi, wt, hs, a, dact, acc):
    n = FF // C
    for c in range(n + 1):
        if c < n:
            hs[c % 2] = nn(n1b[...], wi[:, C * c : C * c + C])
        if c > 0:
            cols = slice(C * (c - 1), C * c)
            v, d = gelu_pair(hs[(c - 1) % 2])
            a[:, cols] = v.astype(BF)
            dact[:, cols] = d
            acc[...] += nn(a[:, cols], wt[cols, :])


def feed_back(gnb, wi, wt, a, dact, acc):
    for c in range(FF // C):
        cols = slice(C * c, C * c + C)
        a[:, cols] = (nt(gnb[...], wt[cols, :]) * dact[:, cols]).astype(BF)
    acc[...] += nt(a[...], wi[...])
def remote(src, dst, send, recv, **where):
    return pltpu.make_async_remote_copy(
        src_ref=src, dst_ref=dst, send_sem=send, recv_sem=recv, device_id=where, device_id_type=MESH
    )


def layer(
    inputs, cot, kmask, lengths, wq, wk, wv, w_out, w_inner, w_outer, g1, b1, g2, b2, dq, uq, dv, uv,
    act_out, ig_out, gd_out, gu_out,
    x, ct, wo, wi, wt, wg, up, act, igb,
    bias, mid, knat, vnat, yt, sscr, p, rl, ctxt, xhat1, xhat2, r1s, n1b, hs, a, dact, acc,
    dot_ref, dosc, dsscr, dkv, dyt, gnb,
    msg, redz, redc, redx, redy, gdp,
    lsem, xsem, csem, wsem, usem, w1, w2, w3, asem, isem, gz, gc, gx, gy, gf,
):
    ix, iy, ic, iz = (lax.axis_index(n) for n in ("dp_0", "dp_1", "dp_2", "heads"))
    rank = lax.rem(iz + 2 * ic, 4)
    owner = rank < 3
    mine = jnp.minimum(rank, 2)

    def z_of(r):
        return lax.rem(r + 2 * ic, 4)

    def turn(i, by):
        return lax.rem(i + by, 4)

    def place(g):
        return turn(iz, g)

    barrier = pltpu.get_barrier_semaphore()
    peers = [{"dp_2": 1 - ic}]
    for i in (1, 2, 3):
        peers += [{"heads": turn(iz, i)}, {"dp_0": turn(ix, i)}, {"dp_1": turn(iy, i)}]
    for where in peers:
        pl.semaphore_signal(barrier, inc=1, device_id=where, device_id_type=MESH)
    weights = (wq, wv, wk)
    loads = [pltpu.make_async_copy(w, wg.at[pl.ds(192 * n, 192)], lsem.at[n]) for n, w in enumerate(weights)]
    late = [
        pltpu.make_async_copy(w, v, lsem.at[3 + n]) for n, (w, v) in enumerate(((w_out, wo), (w_inner, wi), (w_outer, wt)))
    ]
    pl.semaphore_wait(barrier, 10)

    la, lb = ix * (1 - ic) + iy * ic, iy * (1 - ic) + ix * ic
    slice_at = 3 * lb + la
    holds = la < 3

    def part(k, at, count, core=ic):
        rows = pl.ds(pl.multiple_of(GW * k + at, 16), count)
        return wg.at[rows, pl.ds(pl.multiple_of(384 * core, 128), 384)]

    def along_a(i):
        return {"dp_0": turn(ix, i * (1 - ic)), "dp_1": turn(iy, i * ic)}

    def along_b(i):
        return {"dp_0": turn(ix, i * ic), "dp_1": turn(iy, i * (1 - ic))}

    def over_z(i, src=None):
        src = part(0, 48 * slice_at, 48) if src is None else src
        return remote(src, part(4 - i, 48 * slice_at, 48), wsem.at[0, i], wsem.at[1, 4 - i], heads=turn(iz, i))

    def first(k, i):
        block = part(k, 48 * slice_at, 48)
        return remote(block, block, w1.at[0, k, i], w1.at[1, k, i], **along_a(i))

    def second(k, i):
        block = part(k, 144 * lb, 144)
        return remote(block, block, w2.at[0, k, i], w2.at[1, k, i], **along_b(i))

    def third(k, core=ic):
        block = part(k, 0, 576, core)
        return remote(block, block, w3.at[0, k], w3.at[1, k], dp_2=1 - ic)

    def when_holds(do):
        pl.when(holds)(do)

    def join(k):
        for i in (1, 2, 3):
            second(k, i).wait_recv()
        third(k).start()

    for m in range(3):
        @pl.when(jnp.logical_and(holds, slice_at // 4 == m))
        def _():
            rows = pl.ds(pl.multiple_of(48 * lax.rem(slice_at, 4), 16), 48)
            for i in (1, 2, 3):
                over_z(i, weights[m].at[rows, pl.ds(pl.multiple_of(384 * ic, 128), 384)]).start()

    def slot(ref, r):
        return ref.at[pl.ds(pl.multiple_of(r * Q, Q), Q)]

    def spread(src, dst, sem):
        for j in range(B):
            @pl.when(rank != j)
            def _():
                remote(src.at[j], slot(dst, rank), sem.at[0, j], sem.at[1, rank], heads=z_of(j)).start()

            @pl.when(rank == j)
            def _():
                pltpu.make_async_copy(src.at[j], slot(dst, rank), sem.at[1, j]).start()

    def spread_wait(src, dst, sem):
        @pl.when(owner)
        def _():
            for r in range(4):
                pltpu.make_async_copy(src.at[0], dst.at[pl.ds(r * Q, Q)], sem.at[1, r]).wait()

    def spread_end(src, dst, sem):
        for j in range(B):
            @pl.when(rank != j)
            def _():
                remote(src.at[j], slot(dst, rank), sem.at[0, j], sem.at[1, rank], heads=z_of(j)).wait_send()

    spread(inputs, x, xsem)
    for c in loads:
        c.start()

    zero8 = jnp.zeros((8, 192), F32)
    both = jnp.concatenate(
        [
            jnp.concatenate([uq[...].astype(F32), zero8], axis=1),
            jnp.concatenate([zero8, uv[...].astype(F32)], axis=1),
        ],
        axis=0,
    )
    up[0] = (2.0 * both).astype(BF)
    ups = [
        remote(up.at[0], up.at[4 - i], usem.at[0, i], usem.at[1, 4 - i], heads=turn(iz, i)) for i in (1, 2, 3)
    ]
    for c in ups:
        c.start()
    down = jnp.concatenate([dq[...].astype(F32), dv[...].astype(F32)], axis=0).astype(BF)
    for g in range(G):
        wg[GW * g + 576 : GW * g + GW, :] = jnp.concatenate(
            [down if g == 0 else jnp.zeros((16, D), BF), jnp.zeros((48, D), BF)], axis=0
        )

    @when_holds
    def _():
        for k in (1, 2, 3):
            pltpu.make_async_copy(part(k, 0, 48), part(k, 0, 48), wsem.at[1, k]).wait()
            for i in (1, 2, 3):
                first(k, i).start()

    for k in (1, 2, 3):
        for i in (1, 2, 3):
            @pl.when(turn(la, 4 - i) < 3)
            def _():
                first(k, i).wait_recv()
        for i in (1, 2, 3):
            second(k, i).start()
    spread(cot, ct, csem)
    for c in late:
        c.start()

    row = jnp.where(mine == 0, kmask[0:1], jnp.where(mine == 1, kmask[1:2], kmask[2:3]))
    row = jnp.where(ic == 0, row, jnp.concatenate([row[:, 256:512], row[:, 0:256]], axis=1))
    row = jnp.where(row > 0, 0.0, -1e30).astype(F32)
    bias[...] = jnp.where(lax.broadcasted_iota(jnp.int32, (64, S), 0) == 63, row, 0.0).astype(BF)
    for c in loads:
        c.wait()
    for c in ups:
        c.wait_recv()
    join(1)
    spread_wait(inputs, x, xsem)

    def project_group(g):
        project(g, x, wg, up, mid, bias, knat, vnat, yt)

    def attend_some(units):
        attend(units, place, knat, yt, sscr, p, rl, ctxt)

    @pl.when(owner)
    def _():
        middle(x, wg, mid)
        project_group(0)

    for g in range(3):
        if g < 2:
            join(g + 2)
        third(g + 1, 1 - ic).wait_recv()

        @pl.when(owner)
        def _():
            project_group(g + 1)
            attend_some([(g, j, 1) for j in range(3)])

    for c in late:
        c.wait()

    def rows_of(src, t):
        return src.at[pl.ds(pl.multiple_of(t * Q, Q), Q)]

    def sent_back(src, dst, sem, i):
        return remote(rows_of(src, turn(rank, i)), dst.at[mine], sem.at[0, i], sem.at[1, mine], heads=turn(iz, i))

    def back(src, dst, sem):
        for i in (1, 2, 3):
            sent_back(src, dst, sem, i).start()
        pltpu.make_async_copy(rows_of(src, mine), dst.at[mine], sem.at[1, mine]).start()

    def back_end(src, dst, sem):
        for j in range(B):
            pltpu.make_async_copy(src.at[pl.ds(0, Q)], dst.at[j], sem.at[1, j]).wait()

        @pl.when(owner)
        def _():
            for i in (1, 2, 3):
                sent_back(src, dst, sem, i).wait_send()

    @pl.when(owner)
    def _():
        attend_some([(3, j, 1) for j in range(3)] + [(g, j, 0) for g in range(G) for j in range(3)])
        ctx = jnp.concatenate([ctxt[g].T for g in range(G)], axis=1)
        xh, r = norm(x[...].astype(F32) + nn(ctx, wo[...]))
        xhat1[...] = xh
        r1s[...] = r
        n1v = xh * g1[...][None] + b1[...][None]
        n1b[...] = n1v.astype(BF)
        acc[...] = n1v
        feed_forward(n1b, wi, wt, hs, a, dact, acc)
        xh2, r2 = norm(acc[...])
        act[...] = (xh2 * g2[...][None] + b2[...][None]).astype(BF)
        xhat2[...] = xh2
        back(act, act_out, asem)
        acc[:, 0:1] = r2

    spread_wait(cot, ct, csem)

    @pl.when(owner)
    def _():
        limit = lengths[mine]
        at = lax.broadcasted_iota(jnp.int32, (Q, 1), 0)
        valid = jnp.concatenate([at + z_of(t) * Q < limit for t in range(4)], axis=0)
        tangent = jnp.where(valid, ct[...].astype(F32), 0.0)
        gs = norm_back(tangent * g2[...][None], xhat2[...], acc[:, 0:1])
        gnb[...] = gs.astype(BF)
        acc[...] = gs
        feed_back(gnb, wi, wt, a, dact, acc)
        gf1 = norm_back(acc[...] * g1[...][None], xhat1[...], r1s[...])
        acc[...] = gf1
        gfb = gf1.astype(BF)
        for g in range(G):
            dot_ref[g] = nt(wo[192 * g : 192 * g + 192, :], gfb)
        for half in range(2):
            attend_back([(g, j, half) for g in range(G) for j in range(3)], place, vnat, yt, p, rl, ctxt, dot_ref, dosc,
                        dsscr, dkv, dyt)
        gm = jnp.zeros((16, S), F32)
        first_rows = lax.broadcasted_iota(jnp.int32, (16, 192), 0) < 8
        for g in range(G):
            dqv = dyt[GW * g : GW * g + 384, :]
            gu = nt(mid[0:16, :], dqv)
            msg[g, 0:16, 0:192] = jnp.where(first_rows, gu[:, 0:192], gu[:, 192:384]) * 2.0
            gm = gm + nn(up[g], dqv)
        gmb = gm.astype(BF)
        gd = nn(gmb, x[...])
        for q in range(4):
            gdp[q, :, 0:192] = gd[:, 192 * q : 192 * q + 192]
        for k in range(G):
            msg[k, 16:32, 0:192] = gdp[place(k), :, 0:192]
            dyt[GW * k + 576 : GW * k + GW, :] = jnp.concatenate(
                [gmb if k == 0 else jnp.zeros((16, S), BF), jnp.zeros((48, S), BF)], axis=0
            )

    zsum = [remote(msg.at[i], redz.at[4 - i], gz.at[0, i], gz.at[1, 4 - i], heads=turn(iz, i)) for i in (1, 2, 3)]
    core_sum = remote(redz.at[0], redc, gc.at[0], gc.at[1], dp_2=1 - ic)

    def line(buf, sem, axis, me):
        return [remote(buf.at[me], buf.at[me], sem.at[0, i], sem.at[1, i], **{axis: turn(me, i)}) for i in (1, 2, 3)]

    over_x, over_y = line(redx, gx, "dp_0", ix), line(redy, gy, "dp_1", iy)
    over_q = [remote(gd_out.at[iz], gd_out.at[iz], gf.at[0, i], gf.at[1, i], heads=turn(iz, i)) for i in (1, 2, 3)]

    def start(copies):
        for c in copies:
            c.start()

    def finish_copies(copies):
        for c in copies:
            c.wait()

    @pl.when(owner)
    def _():
        start(zsum)
        redz[0] = msg[0]
        for g in range(G):
            a[:, GW * g : GW * g + GW] = dyt[GW * g : GW * g + GW, :].T
        for half in (1, 0):
            rows = half_cols(half)
            igb[rows, :] = (acc[rows, :] + nn(a[rows, 0 : G * GW], wg[...])).astype(BF)
        back(igb, ig_out, isem)

    @pl.when(rank == 3)
    def _():
        redz[0] = jnp.zeros((32, 256), F32)

    for i in (1, 2, 3):
        @pl.when(turn(rank, i) != 3)
        def _():
            pltpu.make_async_copy(msg.at[i], redz.at[i], gz.at[1, i]).wait()
            redz[0] += redz[i]

    core_sum.start()
    core_sum.wait()
    redx[ix] = redz[0] + redc[...]
    start(over_x)
    finish_copies(over_x)
    redy[iy] = redx[0] + redx[1] + redx[2] + redx[3]
    start(over_y)
    finish_copies(over_y)
    total = redy[0] + redy[1] + redy[2] + redy[3]
    gu_out[...] = total[0:16]
    gd_out[iz] = total[16:32]
    start(over_q)
    finish_copies(over_q)

    back_end(act, act_out, asem)
    back_end(igb, ig_out, isem)
    spread_end(inputs, x, xsem)
    spread_end(cot, ct, csem)
    for c in ups:
        c.wait_send()

    @when_holds
    def _():
        for i in (1, 2, 3):
            over_z(i).wait_send()
            for k in (1, 2, 3):
                first(k, i).wait_send()

    for k in (1, 2, 3):
        for i in (1, 2, 3):
            second(k, i).wait_send()
        third(k).wait_send()

    @pl.when(owner)
    def _():
        for c in zsum:
            c.wait_send()


def finish(act_in, ig_in, gd, gu, act, ig, gdq, guq, gdv, guv):
    act[...] = act_in[...]
    ig[...] = ig_in[...].astype(F32)
    down = jnp.concatenate([gd[q, :, 0:192] for q in range(4)], axis=1)
    gdq[...] = down[0:8]
    gdv[...] = down[8:16]
    guq[...] = gu[0:8, 0:192]
    guv[...] = gu[8:16, 0:192]


def scratch():
    V, dma = pltpu.VMEM, pltpu.SemaphoreType.DMA
    return [
        V((S, D), BF), V((S, D), BF), V((D, D), BF), V((D, FF), BF), V((FF, D), BF), V((G * GW, D), BF),
        V((G, 16, 384), BF), V((S, D), BF), V((S, D), BF),
        V((64, S), BF), V((64, S), BF), V((G, S, 256), BF), V((G, S, 256), BF), V((G, GW, S), BF),
        V((3, S, 256), F32), V((12, S, S), BF), V((12, 1, S), F32), V((G, 192, S), BF),
        V((S, D), F32), V((S, D), F32), V((S, 1), F32), V((S, D), BF),
        V((2, S, C), F32), V((S, FF), BF), V((S, FF), F32), V((S, D), F32),
        V((G, 192, S), F32), V((3, 64, 256), BF), V((3, S, 256), BF), V((12, 2, 64, S), F32), V((G * GW, S), BF),
        V((S, D), BF),
        V((4, 32, 256), F32), V((4, 32, 256), F32), V((32, 256), F32), V((4, 32, 256), F32), V((4, 32, 256), F32),
        V((4, 16, 256), F32),
        dma((6,)), dma((2, 4)), dma((2, 4)), dma((2, 4)), dma((2, 4)), dma((2, 4, 4)), dma((2, 4, 4)), dma((2, 4)),
        dma((2, 4)), dma((2, 4)), dma((2, 4)), dma((2,)), dma((2, 4)), dma((2, 4)), dma((2, 4)),
    ]


def per_device(inputs, key_mask, lengths, cotangent, wq, wk, wv, w_out, w_inner, w_outer, g1, b1, g2, b2, dq, uq, dv, uv):
    vm, hbm = pl.BlockSpec(memory_space=pltpu.VMEM), pl.BlockSpec(memory_space=pl.ANY)
    shape = jax.ShapeDtypeStruct
    act, ig, gd, gu = pl.pallas_call(
        layer,
        out_shape=(shape((B, Q, D), BF), shape((B, Q, D), BF), shape((4, 16, 256), F32), shape((16, 256), F32)),
        in_specs=[hbm, hbm, vm, pl.BlockSpec(memory_space=pltpu.SMEM)] + [hbm] * 6 + [vm] * 8,
        out_specs=(hbm, hbm, vm, vm),
        scratch_shapes=scratch(),
        compiler_params=pltpu.CompilerParams(
            collective_id=0, has_side_effects=True, vmem_limit_bytes=62 * 2**20
        ),
    )(
        inputs, cotangent, key_mask, lengths, wq.T, wk.T, wv.T, w_out, w_inner, w_outer,
        g1, b1, g2, b2, dq.T, uq, dv.T, uv,
    )
    act, ig, gdq, guq, gdv, guv = pl.pallas_call(
        finish,
        out_shape=(
            shape((B, Q, D), BF), shape((B, Q, D), F32),
            shape((8, D), F32), shape((8, 192), F32), shape((8, D), F32), shape((8, 192), F32),
        ),
        in_specs=[vm] * 4,
        out_specs=(vm,) * 6,
    )(act, ig, gd, gu)
    return act, ig, gdq.T, guq, gdv.T, guv


def solution(mesh):
    finer = Mesh(
        mesh.devices.reshape(4, 4, 2, mesh.shape["heads"]), ("dp_0", "dp_1", "dp_2", "heads")
    )
    rows, cols, same = P(DP, "heads", None), P(None, "heads"), P()
    return jax.shard_map(
        per_device,
        mesh=finer,
        in_specs=(rows, P(DP, None), P(DP), rows, cols, cols, cols) + (same,) * 8 + (cols, same, cols),
        out_specs=(rows, rows, same, cols, same, cols),
        check_vma=False,
    )
```

```python
import functools

import jax
import jax.numpy as jnp
from jax import lax
from jax.experimental import pallas as pl
from jax.experimental.pallas import tpu as pltpu
from jax.sharding import Mesh
from jax.sharding import PartitionSpec as P

BF, F32 = jnp.bfloat16, jnp.float32
S, D, FF, HD, G = 512, 768, 3072, 64, 4
B, Q = 3, 128
GW = 640
C = 512
NT = (((1,), (1,)), ((), ()))
DP = ("dp_0", "dp_1", "dp_2")
MESH = pl.DeviceIdType.MESH


def nn(a, b):
    return jnp.dot(a, b, preferred_element_type=F32)


def nt(a, b):
    return lax.dot_general(a, b, NT, preferred_element_type=F32)


def middle(x, wg, mid):
    mid[0:16, :] = nt(wg[576:592, :], x[...]).astype(BF)
    mid[16:64, :] = jnp.zeros((48, S), BF)


def project(g, x, wg, up, mid, bias, knat, vnat, yt):
    y = nt(wg[GW * g : GW * g + 576, :], x[...])
    upt = jnp.concatenate([up[g], jnp.zeros((112, 384), BF)], axis=0).T
    qv = y[0:384] + nn(upt[:, 0:64], mid[...])
    vt = qv[192:384].astype(BF)
    yt[g, 0:192, :] = (qv[0:192].astype(BF).astype(F32) * 0.125).astype(BF)
    yt[g, 192:384, :] = vt
    vnat[g] = jnp.concatenate([jnp.zeros((64, S), BF), vt], axis=0).T
    kt = jnp.concatenate([y[384:576].astype(BF), bias[...]], axis=0)
    yt[g, 384:GW, :] = kt
    knat[g] = kt.T


def pad_rows(piece, before, total):
    parts, lanes = [], piece.shape[1]
    if before:
        parts.append(jnp.zeros((before, lanes), BF))
    parts.append(piece)
    after = total - before - piece.shape[0]
    if after:
        parts.append(jnp.zeros((after, lanes), BF))
    return jnp.concatenate(parts, axis=0)


def staged(units, *stages):
    for step in range(len(units) + len(stages) - 1):
        for n, stage in enumerate(stages):
            if 0 <= step - n < len(units):
                stage(step - n, *units[step - n])


def half_cols(half):
    return slice(256 * half, 256 * half + 256)


def attend(units, place, knat, yt, sscr, p, rl, ctxt):
    maxima = {}

    def scores(u, g, j, half):
        cols = half_cols(half)
        last = (lax.broadcasted_iota(jnp.int32, (64, 256), 0) == 63).astype(BF)
        rhs = jnp.concatenate([pad_rows(yt[g, 64 * j : 64 * j + 64, cols], 64 * j, 192), last], axis=0)
        s = nn(knat[g], rhs)
        sscr[u % 3] = s
        maxima[u] = jnp.max(s, axis=0, keepdims=True)

    def weights(u, g, j, half):
        p[g * 3 + j, :, half_cols(half)] = jnp.exp(sscr[u % 3] - maxima[u]).astype(BF)

    def mix(u, g, j, half):
        cols = half_cols(half)
        vt = jnp.concatenate([yt[g, 192 + 64 * j : 256 + 64 * j, :], jnp.ones((16, S), BF)], axis=0)
        ot = nn(vt, p[g * 3 + j, :, cols])
        rinv = 1.0 / ot[64:65]
        rl[g * 3 + j, :, cols] = rinv
        ctxt[place(g), 64 * j : 64 * j + 64, cols] = (ot[0:64] * rinv).astype(BF)

    staged(units, scores, weights, mix)


def attend_back(units, place, vnat, yt, p, rl, ctxt, dot_ref, dosc, dsscr, dkv, dyt):
    def grads(u, g, j, half):
        rows, cols = slice(64 * j, 64 * j + 64), half_cols(half)
        do = (dot_ref[place(g), rows, cols].astype(F32) * rl[g * 3 + j, :, cols]).astype(BF)
        dosc[u % 3] = do
        dsum = jnp.sum(do.astype(F32) * ctxt[place(g), rows, cols].astype(F32), axis=0, keepdims=True)
        dp = nn(vnat[g], pad_rows(do, 64 + 64 * j, 256))
        dsscr[u % 3] = (p[g * 3 + j, :, cols].astype(F32) * (dp - dsum)).astype(BF)

    def products(u, g, j, half):
        h, cols, at = g * 3 + j, half_cols(half), GW * g + 64 * j
        ds = dsscr[u % 3]
        dv = nt(dosc[u % 3], p[h, :, cols])
        dk = nt(yt[g, 64 * j : 64 * j + 64, cols], ds)
        dyt[at : at + 64, cols] = (nn(yt[g, 384 + 64 * j : 448 + 64 * j, :], ds) * 0.125).astype(BF)
        if half == 0:
            dkv[h, 0], dkv[h, 1] = dv, dk
        else:
            dyt[at + 192 : at + 256, :] = (dkv[h, 0] + dv).astype(BF)
            dyt[at + 384 : at + 448, :] = (dkv[h, 1] + dk).astype(BF)

    staged(units, grads, products)


def gelu_pair(v):
    e = jnp.exp(v * v * -0.5)
    t = 1.0 / (1.0 + 0.23164189 * jnp.abs(v))
    tail = t * (0.127414796 + t * (-0.142248368 + t * (0.7107068705 + t * (-0.7265760135 + t * 0.5307027145)))) * e
    cdf = jnp.where(v >= 0.0, 1.0 - tail, tail)
    return v * cdf, cdf + v * (e * 0.3989422804)


def norm(h):
    mean = jnp.mean(h, axis=-1, keepdims=True)
    c = h - mean
    r = lax.rsqrt(jnp.mean(c * c, axis=-1, keepdims=True) + 1e-5)
    return c * r, r


def norm_back(n, xhat, r):
    return r * (n - jnp.mean(n, axis=-1, keepdims=True) - xhat * jnp.mean(n * xhat, axis=-1, keepdims=True))


def chunk(c):
    return pl.ds(pl.multiple_of(c * C, C), C)


def feed_forward(n1b, wi, wt, hs, a, dact, acc):
    n = FF // C
    for c in range(n + 1):
        if c < n:
            hs[c % 2] = nn(n1b[...], wi[:, C * c : C * c + C])
        if c > 0:
            cols = slice(C * (c - 1), C * c)
            v, d = gelu_pair(hs[(c - 1) % 2])
            a[:, cols] = v.astype(BF)
            dact[:, cols] = d
            acc[...] += nn(a[:, cols], wt[cols, :])


def feed_back(gnb, wi, wt, a, dact, acc):
    for c in range(FF // C):
        cols = slice(C * c, C * c + C)
        a[:, cols] = (nt(gnb[...], wt[cols, :]) * dact[:, cols]).astype(BF)
    acc[...] += nt(a[...], wi[...])
def remote(src, dst, send, recv, **where):
    return pltpu.make_async_remote_copy(
        src_ref=src, dst_ref=dst, send_sem=send, recv_sem=recv, device_id=where, device_id_type=MESH
    )


def layer(
    inputs, cot, kmask_in, lengths, wq, wk, wv, w_out, w_inner, w_outer, g1_in, b1_in, g2_in, b2_in, dq_in, uq_in, dv_in, uv_in,
    act_out, ig_out, gd_out, gu_out,
    kmask, g1, b1, g2, b2, dq, uq, dv, uv, x, ct, wo, wi, wt, wg, up, act, igb,
    bias, mid, knat, vnat, yt, sscr, p, rl, ctxt, xhat1, xhat2, r1s, n1b, hs, a, dact, acc,
    dot_ref, dosc, dsscr, dkv, dyt, gnb,
    msg, redz, redx, redy, gdp,
    lsem, xsem, csem, wsem, usem, w1, w2, w3, asem, isem, gz, gx, gy, gf,
):
    ix, iy, ic, iz = (lax.axis_index(n) for n in ("dp_0", "dp_1", "dp_2", "heads"))
    rank = lax.rem(iz + 2 * ic, 4)
    owner = rank < 3
    mine = jnp.minimum(rank, 2)

    def z_of(r):
        return lax.rem(r + 2 * ic, 4)

    def turn(i, by):
        return lax.rem(i + by, 4)

    def turn2(i, by):
        return lax.rem(i + by, 2)

    def place(g):
        return turn(iz, g)

    barrier = pltpu.get_barrier_semaphore()
    peers = [{"dp_2": 1 - ic}]
    for i in (1, 2, 3):
        peers += [{"heads": turn(iz, i)}, {"dp_0": turn(ix, i)}, {"dp_1": turn(iy, i)}]
    peers += [{"heads": turn(iz, i), "dp_2": 1 - ic} for i in (1, 2, 3)]
    for where in peers:
        pl.semaphore_signal(barrier, inc=1, device_id=where, device_id_type=MESH)
    weights = (wq, wv, wk)
    loads = [pltpu.make_async_copy(w, wg.at[pl.ds(192 * n, 192)], lsem.at[n]) for n, w in enumerate(weights)]
    late = [
        pltpu.make_async_copy(w, v, lsem.at[3 + n]) for n, (w, v) in enumerate(((w_out, wo), (w_inner, wi), (w_outer, wt)))
    ]
    small = [
        pltpu.make_async_copy(src, dst, lsem.at[6 + n])
        for n, (src, dst) in enumerate(
            ((kmask_in, kmask), (g1_in, g1), (b1_in, b1), (g2_in, g2), (b2_in, b2),
             (dq_in, dq), (uq_in, uq), (dv_in, dv), (uv_in, uv))
        )
    ]
    for c in loads + small:
        c.start()
    pl.semaphore_wait(barrier, 13)
    for c in loads + small:
        c.wait()

    la, lb = ix * (1 - ic) + iy * ic, iy * (1 - ic) + ix * ic

    def part(k, at, count, core=ic):
        rows = pl.ds(pl.multiple_of(GW * k + at, 16), count)
        return wg.at[rows, pl.ds(pl.multiple_of(384 * core, 128), 384)]

    def block(k, b, half=None, core=ic):
        at, count = ((0, 144), (0, 80), (80, 64))[0 if half is None else half + 1]
        return part(k, 144 * b + at, count, core)

    def along_a(i):
        return {"dp_0": turn(ix, i * (1 - ic)), "dp_1": turn(iy, i * ic)}

    def along_b(i):
        return {"dp_0": turn(ix, i * ic), "dp_1": turn(iy, i * (1 - ic))}

    over_z = remote(block(0, lb), block(la, lb), wsem.at[0], wsem.at[1], heads=turn(iz, 4 - la))

    def ring_a(n, k):
        what = block(k, lb, n - 2 if n > 1 else None)
        return remote(what, what, w1.at[0, n], w1.at[1, n], **along_a(3 if n % 2 else 1))

    def ring_b(n, k, b):
        what = block(k, b, n - 2 if n > 1 else None)
        return remote(what, what, w2.at[0, n, k], w2.at[1, n, k], **along_b(3 if n % 2 else 1))

    def to_core(k, b, core=ic):
        what = block(k, b, None, core)
        return remote(what, what, w3.at[0, k, b], w3.at[1, k, b], dp_2=1 - ic)

    def got_line(k):
        ring_b(0, k, lb).start()
        ring_b(1, k, lb).start()
        to_core(k, lb).start()

    def join_line():
        @pl.when(la > 0)
        def _():
            over_z.wait_recv()
            ring_a(0, la).start()
            ring_a(1, la).start()
            got_line(la)

        for n, k in ((0, turn(la, 3)), (1, turn(la, 1))):
            @pl.when(k > 0)
            def _():
                ring_a(n, k).wait_recv()
                ring_a(n + 2, k).start()
                got_line(k)

        far = turn(la, 2)

        @pl.when(far > 0)
        def _():
            ring_a(2, far).wait_recv()
            ring_a(3, far).wait_recv()
            got_line(far)

    def join(k):
        for n, b in ((0, turn(lb, 3)), (1, turn(lb, 1))):
            ring_b(n, k, b).wait_recv()
            ring_b(n + 2, k, b).start()
            to_core(k, b).start()
        far = turn(lb, 2)
        ring_b(2, k, far).wait_recv()
        ring_b(3, k, far).wait_recv()
        to_core(k, far).start()

    def arrived(k):
        for b in range(4):
            to_core(k, b, 1 - ic).wait_recv()

    def weights_end():
        @pl.when(la > 0)
        def _():
            over_z.wait_send()
            ring_a(0, la).wait_send()
            ring_a(1, la).wait_send()

        for n, k in ((0, turn(la, 3)), (1, turn(la, 1))):
            @pl.when(k > 0)
            def _():
                ring_a(n + 2, k).wait_send()

        for k in (1, 2, 3):
            for n in range(4):
                ring_b(n, k, lb).wait_send()
            for b in range(4):
                to_core(k, b).wait_send()

    @pl.when(la > 0)
    def _():
        over_z.start()

    def slot(ref, r):
        return ref.at[pl.ds(pl.multiple_of(r * Q, Q), Q)]

    def spread(src, dst, sem):
        for j in range(B):
            @pl.when(rank != j)
            def _():
                remote(src.at[j], slot(dst, rank), sem.at[0, j], sem.at[1, rank], heads=z_of(j)).start()

            @pl.when(rank == j)
            def _():
                pltpu.make_async_copy(src.at[j], slot(dst, rank), sem.at[1, j]).start()

    def spread_wait(src, dst, sem):
        @pl.when(owner)
        def _():
            for r in range(4):
                pltpu.make_async_copy(src.at[0], dst.at[pl.ds(r * Q, Q)], sem.at[1, r]).wait()

    def spread_end(src, dst, sem):
        for j in range(B):
            @pl.when(rank != j)
            def _():
                remote(src.at[j], slot(dst, rank), sem.at[0, j], sem.at[1, rank], heads=z_of(j)).wait_send()

    spread(inputs, x, xsem)

    zero8 = jnp.zeros((8, 192), F32)
    both = jnp.concatenate(
        [
            jnp.concatenate([uq[...].astype(F32), zero8], axis=1),
            jnp.concatenate([zero8, uv[...].astype(F32)], axis=1),
        ],
        axis=0,
    )
    up[0] = (2.0 * both).astype(BF)
    ups = [
        remote(up.at[0], up.at[4 - i], usem.at[0, i], usem.at[1, 4 - i], heads=turn(iz, i)) for i in (1, 2, 3)
    ]
    for c in ups:
        c.start()
    down = jnp.concatenate([dq[...].astype(F32), dv[...].astype(F32)], axis=0).astype(BF)
    for g in range(G):
        wg[GW * g + 576 : GW * g + GW, :] = jnp.concatenate(
            [down if g == 0 else jnp.zeros((16, D), BF), jnp.zeros((48, D), BF)], axis=0
        )

    join_line()
    spread(cot, ct, csem)
    for c in late:
        c.start()

    row = jnp.where(mine == 0, kmask[0:1], jnp.where(mine == 1, kmask[1:2], kmask[2:3]))
    row = jnp.where(ic == 0, row, jnp.concatenate([row[:, 256:512], row[:, 0:256]], axis=1))
    row = jnp.where(row > 0, 0.0, -1e30).astype(F32)
    bias[...] = jnp.where(lax.broadcasted_iota(jnp.int32, (64, S), 0) == 63, row, 0.0).astype(BF)
    for c in ups:
        c.wait_recv()
    join(1)
    spread_wait(inputs, x, xsem)

    def project_group(g):
        project(g, x, wg, up, mid, bias, knat, vnat, yt)

    def attend_some(units):
        attend(units, place, knat, yt, sscr, p, rl, ctxt)

    @pl.when(owner)
    def _():
        middle(x, wg, mid)
        project_group(0)

    for g in range(3):
        if g < 2:
            join(g + 2)
        arrived(g + 1)

        @pl.when(owner)
        def _():
            project_group(g + 1)
            attend_some([(g, j, half) for half in (1, 0) for j in range(3)])

    for c in late:
        c.wait()

    def rows_of(src, t):
        return src.at[pl.ds(pl.multiple_of(t * Q, Q), Q)]

    def sent_back(src, dst, sem, i):
        return remote(rows_of(src, turn(rank, i)), dst.at[mine], sem.at[0, i], sem.at[1, mine], heads=turn(iz, i))

    def back(src, dst, sem):
        for i in (1, 2, 3):
            sent_back(src, dst, sem, i).start()
        pltpu.make_async_copy(rows_of(src, mine), dst.at[mine], sem.at[1, mine]).start()

    def back_end(src, dst, sem):
        for j in range(B):
            pltpu.make_async_copy(src.at[pl.ds(0, Q)], dst.at[j], sem.at[1, j]).wait()

        @pl.when(owner)
        def _():
            for i in (1, 2, 3):
                sent_back(src, dst, sem, i).wait_send()

    @pl.when(owner)
    def _():
        attend_some([(3, j, half) for half in (1, 0) for j in range(3)])
        ctx = jnp.concatenate([ctxt[g].T for g in range(G)], axis=1)
        xh, r = norm(x[...].astype(F32) + nn(ctx, wo[...]))
        xhat1[...] = xh
        r1s[...] = r
        n1v = xh * g1[...][None] + b1[...][None]
        n1b[...] = n1v.astype(BF)
        acc[...] = n1v
        feed_forward(n1b, wi, wt, hs, a, dact, acc)
        xh2, r2 = norm(acc[...])
        act[...] = (xh2 * g2[...][None] + b2[...][None]).astype(BF)
        xhat2[...] = xh2
        back(act, act_out, asem)
        acc[:, 0:1] = r2

    spread_wait(cot, ct, csem)

    @pl.when(owner)
    def _():
        limit = lengths[mine]
        at = lax.broadcasted_iota(jnp.int32, (Q, 1), 0)
        valid = jnp.concatenate([at + z_of(t) * Q < limit for t in range(4)], axis=0)
        tangent = jnp.where(valid, ct[...].astype(F32), 0.0)
        gs = norm_back(tangent * g2[...][None], xhat2[...], acc[:, 0:1])
        gnb[...] = gs.astype(BF)
        acc[...] = gs
        feed_back(gnb, wi, wt, a, dact, acc)
        gf1 = norm_back(acc[...] * g1[...][None], xhat1[...], r1s[...])
        acc[...] = gf1
        gfb = gf1.astype(BF)
        for g in range(G):
            dot_ref[g] = nt(wo[192 * g : 192 * g + 192, :], gfb)
        for half in range(2):
            attend_back([(g, j, half) for g in range(G) for j in range(3)], place, vnat, yt, p, rl, ctxt, dot_ref, dosc,
                        dsscr, dkv, dyt)
        gm = jnp.zeros((16, S), F32)
        first_rows = lax.broadcasted_iota(jnp.int32, (16, 192), 0) < 8
        for g in range(G):
            dqv = dyt[GW * g : GW * g + 384, :]
            gu = nt(mid[0:16, :], dqv)
            msg[g, 0:16, 0:192] = jnp.where(first_rows, gu[:, 0:192], gu[:, 192:384]) * 2.0
            gm = gm + nn(up[g], dqv)
        gmb = gm.astype(BF)
        gd = nn(gmb, x[...])
        for q in range(4):
            gdp[q, :, 0:192] = gd[:, 192 * q : 192 * q + 192]
        for k in range(G):
            msg[k, 16:32, 0:192] = gdp[place(k), :, 0:192]
            dyt[GW * k + 576 : GW * k + GW, :] = jnp.concatenate(
                [gmb if k == 0 else jnp.zeros((16, S), BF), jnp.zeros((48, S), BF)], axis=0
            )

    zsum = [
        remote(msg.at[i], redz.at[ic, iz], gz.at[0, o, i], gz.at[1, ic, iz], heads=turn(iz, i), dp_2=turn2(ic, o))
        for o in (0, 1) for i in range(4) if o + i > 0
    ]

    def line(buf, sem, axis, me):
        return [remote(buf.at[me], buf.at[me], sem.at[0, i], sem.at[1, i], **{axis: turn(me, i)}) for i in (1, 2, 3)]

    over_x, over_y = line(redx, gx, "dp_0", ix), line(redy, gy, "dp_1", iy)
    over_q = [remote(gd_out.at[iz], gd_out.at[iz], gf.at[0, i], gf.at[1, i], heads=turn(iz, i)) for i in (1, 2, 3)]

    def start(copies):
        for c in copies:
            c.start()

    def finish_copies(copies):
        for c in copies:
            c.wait()

    def last_product(half):
        rows = half_cols(half)
        igb[rows, :] = (acc[rows, :] + nn(a[rows, 0 : G * GW], wg[...])).astype(BF)

    @pl.when(owner)
    def _():
        start(zsum)
        redz[ic, iz] = msg[0]
        for g in range(G):
            a[:, GW * g : GW * g + GW] = dyt[GW * g : GW * g + GW, :].T
        last_product(1)

    total = jnp.zeros((32, 256), F32)
    for c in range(2):
        for z in range(4):
            if (z + 2 * c) % 4 != 3:
                @pl.when(jnp.logical_or(ic != c, iz != z))
                def _():
                    pltpu.make_async_copy(msg.at[0], redz.at[c, z], gz.at[1, c, z]).wait()
                total = total + redz[c, z]
    redx[ix] = total
    start(over_x)

    @pl.when(owner)
    def _():
        last_product(0)
        back(igb, ig_out, isem)

    finish_copies(over_x)
    redy[iy] = redx[0] + redx[1] + redx[2] + redx[3]
    start(over_y)
    finish_copies(over_y)
    total = redy[0] + redy[1] + redy[2] + redy[3]
    gu_out[...] = total[0:16]
    gd_out[iz] = total[16:32]
    start(over_q)
    finish_copies(over_q)

    back_end(act, act_out, asem)
    back_end(igb, ig_out, isem)
    spread_end(inputs, x, xsem)
    spread_end(cot, ct, csem)
    for c in ups:
        c.wait_send()

    weights_end()

    @pl.when(owner)
    def _():
        for c in zsum:
            c.wait_send()


def finish(act_in, ig_in, gd, gu, act, ig, gdq, guq, gdv, guv):
    act[...] = act_in[...]
    ig[...] = ig_in[...].astype(F32)
    down = jnp.concatenate([gd[q, :, 0:192] for q in range(4)], axis=1)
    gdq[...] = down[0:8]
    gdv[...] = down[8:16]
    guq[...] = gu[0:8, 0:192]
    guv[...] = gu[8:16, 0:192]


def scratch():
    V, dma = pltpu.VMEM, pltpu.SemaphoreType.DMA
    return [
        V((B, S), jnp.int32), V((D,), F32), V((D,), F32), V((D,), F32), V((D,), F32),
        V((8, D), BF), V((8, 192), BF), V((8, D), BF), V((8, 192), BF),
        V((S, D), BF), V((S, D), BF), V((D, D), BF), V((D, FF), BF), V((FF, D), BF), V((G * GW, D), BF),
        V((G, 16, 384), BF), V((S, D), BF), V((S, D), BF),
        V((64, S), BF), V((64, S), BF), V((G, S, 256), BF), V((G, S, 256), BF), V((G, GW, S), BF),
        V((3, S, 256), F32), V((12, S, S), BF), V((12, 1, S), F32), V((G, 192, S), BF),
        V((S, D), F32), V((S, D), F32), V((S, 1), F32), V((S, D), BF),
        V((2, S, C), F32), V((S, FF), BF), V((S, FF), F32), V((S, D), F32),
        V((G, 192, S), F32), V((3, 64, 256), BF), V((3, S, 256), BF), V((12, 2, 64, S), F32), V((G * GW, S), BF),
        V((S, D), BF),
        V((4, 32, 256), F32), V((2, 4, 32, 256), F32), V((4, 32, 256), F32), V((4, 32, 256), F32),
        V((4, 16, 256), F32),
        dma((15,)), dma((2, 4)), dma((2, 4)), dma((2,)), dma((2, 4)), dma((2, 4)), dma((2, 4, 4)), dma((2, 4, 4)),
        dma((2, 4)), dma((2, 4)), dma((2, 2, 4)), dma((2, 4)), dma((2, 4)), dma((2, 4)),
    ]


def per_device(inputs, key_mask, lengths, cotangent, wq, wk, wv, w_out, w_inner, w_outer, g1, b1, g2, b2, dq, uq, dv, uv):
    vm, hbm = pl.BlockSpec(memory_space=pltpu.VMEM), pl.BlockSpec(memory_space=pl.ANY)
    shape = jax.ShapeDtypeStruct
    act, ig, gd, gu = pl.pallas_call(
        layer,
        out_shape=(shape((B, Q, D), BF), shape((B, Q, D), BF), shape((4, 16, 256), F32), shape((16, 256), F32)),
        in_specs=[hbm] * 3 + [pl.BlockSpec(memory_space=pltpu.SMEM)] + [hbm] * 14,
        out_specs=(hbm, hbm, vm, vm),
        scratch_shapes=scratch(),
        compiler_params=pltpu.CompilerParams(
            collective_id=0, has_side_effects=True, vmem_limit_bytes=62 * 2**20
        ),
    )(
        inputs, cotangent, key_mask, lengths, wq.T, wk.T, wv.T, w_out, w_inner, w_outer,
        g1, b1, g2, b2, dq.T, uq, dv.T, uv,
    )
    act, ig, gdq, guq, gdv, guv = pl.pallas_call(
        finish,
        out_shape=(
            shape((B, Q, D), BF), shape((B, Q, D), F32),
            shape((8, D), F32), shape((8, 192), F32), shape((8, D), F32), shape((8, 192), F32),
        ),
        in_specs=[vm] * 4,
        out_specs=(vm,) * 6,
    )(act, ig, gd, gu)
    return act, ig, gdq.T, guq, gdv.T, guv


def solution(mesh):
    finer = Mesh(
        mesh.devices.reshape(4, 4, 2, mesh.shape["heads"]), ("dp_0", "dp_1", "dp_2", "heads")
    )
    rows, cols, same = P(DP, "heads", None), P(None, "heads"), P()
    return jax.shard_map(
        per_device,
        mesh=finer,
        in_specs=(rows, P(DP, None), P(DP), rows, cols, cols, cols) + (same,) * 8 + (cols, same, cols),
        out_specs=(rows, rows, same, cols, same, cols),
        check_vma=False,
    )
```

```python
import functools

import jax
import jax.numpy as jnp
from jax import lax
from jax.experimental import pallas as pl
from jax.experimental.pallas import tpu as pltpu
from jax.sharding import Mesh
from jax.sharding import PartitionSpec as P

BF, F32 = jnp.bfloat16, jnp.float32
S, D, FF, HD, G = 512, 768, 3072, 64, 4
B, Q = 3, 128
GW = 640
C = 512
NT = (((1,), (1,)), ((), ()))
DP = ("dp_0", "dp_1", "dp_2")
MESH = pl.DeviceIdType.MESH


def nn(a, b):
    return jnp.dot(a, b, preferred_element_type=F32)


def nt(a, b):
    return lax.dot_general(a, b, NT, preferred_element_type=F32)


def middle(x, wg, mid):
    mid[0:16, :] = nt(wg[576:592, :], x[...]).astype(BF)
    mid[16:64, :] = jnp.zeros((48, S), BF)


def project(g, x, wg, up, mid, bias, knat, vnat, yt):
    y = nt(wg[GW * g : GW * g + 576, :], x[...])
    upt = jnp.concatenate([up[g], jnp.zeros((112, 384), BF)], axis=0).T
    qv = y[0:384] + nn(upt[:, 0:64], mid[...])
    vt = qv[192:384].astype(BF)
    yt[g, 0:192, :] = (qv[0:192].astype(BF).astype(F32) * 0.125).astype(BF)
    yt[g, 192:384, :] = vt
    vnat[g] = jnp.concatenate([jnp.zeros((64, S), BF), vt], axis=0).T
    kt = jnp.concatenate([y[384:576].astype(BF), bias[...]], axis=0)
    yt[g, 384:GW, :] = kt
    knat[g] = kt.T


def pad_rows(piece, before, total):
    parts, lanes = [], piece.shape[1]
    if before:
        parts.append(jnp.zeros((before, lanes), BF))
    parts.append(piece)
    after = total - before - piece.shape[0]
    if after:
        parts.append(jnp.zeros((after, lanes), BF))
    return jnp.concatenate(parts, axis=0)


def staged(units, *stages):
    for step in range(len(units) + len(stages) - 1):
        for n, stage in enumerate(stages):
            if 0 <= step - n < len(units):
                stage(step - n, *units[step - n])


def half_cols(half):
    return slice(256 * half, 256 * half + 256)


def attend(units, place, knat, yt, sscr, p, rl, ctxt):
    maxima = {}

    def scores(u, g, j, half):
        cols = half_cols(half)
        last = (lax.broadcasted_iota(jnp.int32, (64, 256), 0) == 63).astype(BF)
        rhs = jnp.concatenate([pad_rows(yt[g, 64 * j : 64 * j + 64, cols], 64 * j, 192), last], axis=0)
        s = nn(knat[g], rhs)
        sscr[u % 3] = s
        maxima[u] = jnp.max(s, axis=0, keepdims=True)

    def weights(u, g, j, half):
        p[g * 3 + j, :, half_cols(half)] = jnp.exp(sscr[u % 3] - maxima[u]).astype(BF)

    def mix(u, g, j, half):
        cols = half_cols(half)
        vt = jnp.concatenate([yt[g, 192 + 64 * j : 256 + 64 * j, :], jnp.ones((16, S), BF)], axis=0)
        ot = nn(vt, p[g * 3 + j, :, cols])
        rinv = 1.0 / ot[64:65]
        rl[g * 3 + j, :, cols] = rinv
        ctxt[place(g), 64 * j : 64 * j + 64, cols] = (ot[0:64] * rinv).astype(BF)

    staged(units, scores, weights, mix)


def attend_back(units, place, vnat, yt, p, rl, ctxt, dot_ref, dosc, dyt, group_done):
    def values(u, g, j):
        rows, h = slice(64 * j, 64 * j + 64), g * 3 + j
        do = (dot_ref[place(g), rows, :] * rl[h]).astype(BF)
        dosc[u % 3] = do
        dyt[g, 192 + 64 * j : 256 + 64 * j, :] = nt(do, p[h]).astype(BF)

    def scores(u, g, j):
        rows, h = slice(64 * j, 64 * j + 64), g * 3 + j
        for half in range(2):
            cols = half_cols(half)
            do = dosc[u % 3, :, cols]
            dsum = jnp.sum(do.astype(F32) * ctxt[place(g), rows, cols].astype(F32), axis=0, keepdims=True)
            dp = nn(vnat[g], pad_rows(do, 64 + 64 * j, 256))
            p[h, :, cols] = (p[h, :, cols].astype(F32) * (dp - dsum)).astype(BF)

    def queries(u, g, j):
        ds = p[g * 3 + j]
        dyt[g, 64 * j : 64 * j + 64, :] = (nn(yt[g, 384 + 64 * j : 448 + 64 * j, :], ds) * 0.125).astype(BF)
        if j == 2:
            group_done(g)

    staged(units, values, scores, queries)


def gelu_pair(v):
    e = jnp.exp(v * v * -0.5)
    t = 1.0 / (1.0 + 0.23164189 * jnp.abs(v))
    tail = t * (0.127414796 + t * (-0.142248368 + t * (0.7107068705 + t * (-0.7265760135 + t * 0.5307027145)))) * e
    cdf = jnp.where(v >= 0.0, 1.0 - tail, tail)
    return v * cdf, cdf + v * (e * 0.3989422804)


def norm(h):
    mean = jnp.mean(h, axis=-1, keepdims=True)
    c = h - mean
    r = lax.rsqrt(jnp.mean(c * c, axis=-1, keepdims=True) + 1e-5)
    return c * r, r


def norm_back(n, xhat, r):
    return r * (n - jnp.mean(n, axis=-1, keepdims=True) - xhat * jnp.mean(n * xhat, axis=-1, keepdims=True))


def chunk(c):
    return pl.ds(pl.multiple_of(c * C, C), C)


def feed_forward(n1b, wi, wt, hs, a, dact, acc):
    n = FF // C
    for c in range(n + 2):
        if c < n:
            hs[c % 2] = nn(n1b[...], wi[:, C * c : C * c + C])
        if 0 < c <= n:
            cols = slice(C * (c - 1), C * c)
            v, d = gelu_pair(hs[(c - 1) % 2])
            a[:, cols] = v.astype(BF)
            dact[:, cols] = d
        if c > 1:
            cols = slice(C * (c - 2), C * (c - 1))
            acc[...] += nn(a[:, cols], wt[cols, :])


def feed_back(gnb, wi, wt, a, dact, acc):
    for c in range(FF // C):
        cols = slice(C * c, C * c + C)
        a[:, cols] = (nt(gnb[...], wt[cols, :]) * dact[:, cols]).astype(BF)
    acc[...] += nt(a[...], wi[...])
def remote(src, dst, send, recv, **where):
    return pltpu.make_async_remote_copy(
        src_ref=src, dst_ref=dst, send_sem=send, recv_sem=recv, device_id=where, device_id_type=MESH
    )


def layer(
    inputs, cot, kmask_in, lengths, wq, wk, wv, w_out, w_inner, w_outer, g1_in, b1_in, g2_in, b2_in, dq_in, uq_in, dv_in, uv_in,
    act_out, ig_out, gd_out, gu_out,
    kmask, g1, b1, g2, b2, dq, uq, dv, uv, x, ct, wo, wi, wt, wg, up, act, igb,
    bias, mid, knat, vnat, yt, sscr, p, rl, ctxt, xhat1, xhat2, r1s, n1b, hs, a, dact, acc,
    dot_ref, dosc, dyt, gnb,
    msg, redz, redx, redy, gmid,
    lsem, xsem, csem, wsem, usem, w1, w2, w3, asem, isem, gz, gx, gy,
):
    ix, iy, ic, iz = (lax.axis_index(n) for n in ("dp_0", "dp_1", "dp_2", "heads"))
    rank = lax.rem(iz + 2 * ic, 4)
    owner = rank < 3
    mine = jnp.minimum(rank, 2)

    def z_of(r):
        return lax.rem(r + 2 * ic, 4)

    def turn(i, by):
        return lax.rem(i + by, 4)

    def turn2(i, by):
        return lax.rem(i + by, 2)

    def place(g):
        return turn(iz, g)

    barrier = pltpu.get_barrier_semaphore()
    peers = [{"dp_2": 1 - ic}]
    for i in (1, 2, 3):
        peers += [{"heads": turn(iz, i)}, {"dp_0": turn(ix, i)}, {"dp_1": turn(iy, i)}]
    for i in (1, 2, 3):
        peers += [{"heads": turn(iz, i), "dp_2": 1 - ic}, {"dp_1": turn(iy, i), "dp_2": 1 - ic}]
    for where in peers:
        pl.semaphore_signal(barrier, inc=1, device_id=where, device_id_type=MESH)
    weights = (wq, wv, wk)
    loads = [pltpu.make_async_copy(w, wg.at[pl.ds(192 * n, 192)], lsem.at[n]) for n, w in enumerate(weights)]
    late = [
        pltpu.make_async_copy(w, v, lsem.at[3 + n]) for n, (w, v) in enumerate(((w_out, wo), (w_inner, wi), (w_outer, wt)))
    ]
    small = [
        pltpu.make_async_copy(src, dst, lsem.at[6 + n])
        for n, (src, dst) in enumerate(
            ((kmask_in, kmask), (g1_in, g1), (b1_in, b1), (g2_in, g2), (b2_in, b2),
             (dq_in, dq), (uq_in, uq), (dv_in, dv), (uv_in, uv))
        )
    ]
    for c in loads + small:
        c.start()
    pl.semaphore_wait(barrier, 16)
    for c in loads:
        c.wait()

    la, lb = ix * (1 - ic) + iy * ic, iy * (1 - ic) + ix * ic
    holds = la < 3

    def part(k, at, count, core=ic):
        rows = pl.ds(pl.multiple_of(GW * k + at, 16), count)
        return wg.at[rows, pl.ds(pl.multiple_of(384 * core, 128), 384)]

    def piece(k, a):
        return part(k, 48 * (3 * lb + a), 48)

    def along_a(i):
        return {"dp_0": turn(ix, i * (1 - ic)), "dp_1": turn(iy, i * ic)}

    def along_b(i):
        return {"dp_0": turn(ix, i * ic), "dp_1": turn(iy, i * (1 - ic))}

    def over_z(i):
        return remote(piece(0, la), piece(4 - i, la), wsem.at[0, i], wsem.at[1, 4 - i], heads=turn(iz, i))

    def first(k, i):
        return remote(piece(k, la), piece(k, la), w1.at[0, k, i], w1.at[1, k, i], **along_a(i))

    def second(k, a, i):
        return remote(piece(k, a), piece(k, a), w2.at[0, k, a, i], w2.at[1, k, a, i], **along_b(i))

    def third(k, core=ic):
        what = part(k, 0, 576, core)
        return remote(what, what, w3.at[0, k], w3.at[1, k], dp_2=1 - ic)

    def join_line():
        @pl.when(holds)
        def _():
            for k in (1, 2, 3):
                over_z(4 - k).wait_recv()
                for i in (1, 2, 3):
                    first(k, i).start()
                    second(k, la, i).start()

        for k in (1, 2, 3):
            for i in (1, 2, 3):
                source = turn(la, 4 - i)

                @pl.when(source < 3)
                def _():
                    first(k, i).wait_recv()
                    for n in (1, 2, 3):
                        second(k, source, n).start()

    def join(k):
        for a in range(3):
            for i in (1, 2, 3):
                second(k, a, i).wait_recv()
        third(k).start()

    def arrived(k):
        third(k, 1 - ic).wait_recv()

    def weights_end():
        @pl.when(holds)
        def _():
            for i in (1, 2, 3):
                over_z(i).wait_send()
                for k in (1, 2, 3):
                    first(k, i).wait_send()

        for k in (1, 2, 3):
            for a in range(3):
                for i in (1, 2, 3):
                    second(k, a, i).wait_send()
            third(k).wait_send()

    @pl.when(holds)
    def _():
        for i in (1, 3, 2):
            over_z(i).start()

    def slot(ref, r):
        return ref.at[pl.ds(pl.multiple_of(r * Q, Q), Q)]

    def spread_to(src, dst, sem, i):
        j = jnp.minimum(turn(rank, i), 2)
        return remote(src.at[j], slot(dst, rank), sem.at[0, i], sem.at[1, rank], heads=turn(iz, i))

    def spread(src, dst, sem):
        for i in (2, 1, 3):
            pl.when(turn(rank, i) < 3)(spread_to(src, dst, sem, i).start)

        @pl.when(owner)
        def _():
            pltpu.make_async_copy(src.at[mine], slot(dst, mine), sem.at[1, mine]).start()

    def spread_wait(src, dst, sem):
        @pl.when(owner)
        def _():
            for r in range(4):
                pltpu.make_async_copy(src.at[0], dst.at[pl.ds(r * Q, Q)], sem.at[1, r]).wait()

    def spread_end(src, dst, sem):
        for i in (1, 2, 3):
            pl.when(turn(rank, i) < 3)(spread_to(src, dst, sem, i).wait_send)

    spread(inputs, x, xsem)

    for c in small:
        c.wait()
    zero8 = jnp.zeros((8, 192), F32)
    both = jnp.concatenate(
        [
            jnp.concatenate([uq[...].astype(F32), zero8], axis=1),
            jnp.concatenate([zero8, uv[...].astype(F32)], axis=1),
        ],
        axis=0,
    )
    up[0] = (2.0 * both).astype(BF)
    ups = [
        remote(up.at[0], up.at[4 - i], usem.at[0, i], usem.at[1, 4 - i], heads=turn(iz, i)) for i in (1, 2, 3)
    ]
    for c in ups:
        c.start()
    down = jnp.concatenate([dq[...].astype(F32), dv[...].astype(F32)], axis=0).astype(BF)
    for g in range(G):
        wg[GW * g + 576 : GW * g + GW, :] = jnp.concatenate(
            [down if g == 0 else jnp.zeros((16, D), BF), jnp.zeros((48, D), BF)], axis=0
        )

    join_line()
    spread(cot, ct, csem)
    for c in late:
        c.start()

    row = jnp.where(mine == 0, kmask[0:1], jnp.where(mine == 1, kmask[1:2], kmask[2:3]))
    row = jnp.where(ic == 0, row, jnp.concatenate([row[:, 256:512], row[:, 0:256]], axis=1))
    row = jnp.where(row > 0, 0.0, -1e30).astype(F32)
    bias[...] = jnp.where(lax.broadcasted_iota(jnp.int32, (64, S), 0) == 63, row, 0.0).astype(BF)
    for c in ups:
        c.wait_recv()
    join(1)
    spread_wait(inputs, x, xsem)

    def project_group(g):
        project(g, x, wg, up, mid, bias, knat, vnat, yt)

    def attend_some(units):
        attend(units, place, knat, yt, sscr, p, rl, ctxt)

    @pl.when(owner)
    def _():
        middle(x, wg, mid)
        project_group(0)

    for g in range(3):
        if g < 2:
            join(g + 2)
        arrived(g + 1)

        @pl.when(owner)
        def _():
            project_group(g + 1)
            attend_some([(g, j, half) for half in (1, 0) for j in range(3)])

    for c in late:
        c.wait()

    def rows_of(src, t):
        return src.at[pl.ds(pl.multiple_of(t * Q, Q), Q)]

    def sent_back(src, dst, sem, i):
        return remote(rows_of(src, turn(rank, i)), dst.at[mine], sem.at[0, i], sem.at[1, mine], heads=turn(iz, i))

    def own_back(src, dst, sem):
        return pltpu.make_async_copy(rows_of(src, mine), dst.at[mine], sem.at[1, mine])

    def back(src, dst, sem):
        for i in (1, 2, 3):
            sent_back(src, dst, sem, i).start()
        own_back(src, dst, sem).start()

    def back_end(src, dst, sem):
        for j in range(B):
            pltpu.make_async_copy(src.at[pl.ds(0, Q)], dst.at[j], sem.at[1, j]).wait()

        @pl.when(owner)
        def _():
            for i in (1, 2, 3):
                sent_back(src, dst, sem, i).wait_send()

    @pl.when(owner)
    def _():
        attend_some([(3, j, half) for half in (1, 0) for j in range(3)])
        ctx = jnp.concatenate([ctxt[g].T for g in range(G)], axis=1)
        xh, r = norm(x[...].astype(F32) + nn(ctx, wo[...]))
        xhat1[...] = xh
        r1s[...] = r
        n1v = xh * g1[...][None] + b1[...][None]
        n1b[...] = n1v.astype(BF)
        acc[...] = n1v
        feed_forward(n1b, wi, wt, hs, a, dact, acc)
        xh2, r2 = norm(acc[...])
        act[...] = (xh2 * g2[...][None] + b2[...][None]).astype(BF)
        xhat2[...] = xh2
        back(act, act_out, asem)
        acc[:, 0:1] = r2

    spread_wait(cot, ct, csem)

    @pl.when(owner)
    def _():
        limit = lengths[mine]
        at = lax.broadcasted_iota(jnp.int32, (Q, 1), 0)
        valid = jnp.concatenate([at + z_of(t) * Q < limit for t in range(4)], axis=0)
        tangent = jnp.where(valid, ct[...].astype(F32), 0.0)
        gs = norm_back(tangent * g2[...][None], xhat2[...], acc[:, 0:1])
        gnb[...] = gs.astype(BF)
        acc[...] = gs
        feed_back(gnb, wi, wt, a, dact, acc)
        gf1 = norm_back(acc[...] * g1[...][None], xhat1[...], r1s[...])
        acc[...] = gf1
        gfb = gf1.astype(BF)
        for g in range(G):
            dot_ref[g] = nt(wo[192 * g : 192 * g + 192, :], gfb)
        middle_sum = [jnp.zeros((16, S), F32)]
        first_rows = lax.broadcasted_iota(jnp.int32, (16, 192), 0) < 8

        def group_done(g):
            dqv = dyt[g]
            a[:, GW * g : GW * g + 384] = dqv.T
            gu = nt(mid[0:16, :], dqv)
            gu = jnp.where(first_rows, gu[:, 0:192], gu[:, 192:384]) * 2.0
            msg[g, 1, :, 256:512] = jnp.concatenate([gu, jnp.zeros((16, 64), F32)], axis=1).astype(BF)
            middle_sum[0] = middle_sum[0] + nn(up[g], dqv)

        attend_back([(g, j) for g in range(G) for j in range(3)], place, vnat, yt, p, rl, ctxt, dot_ref, dosc, dyt, group_done)
        gmb = middle_sum[0].astype(BF)
        gmid[0:16, :] = gmb
        gmid[16:64, :] = jnp.zeros((48, S), BF)
        gd = nn(gmb, x[...]).astype(BF)
        for g in range(G):
            msg[g, 0] = gd[:, 0:512]
            msg[g, 1, :, 0:256] = gd[:, 512:768]

    zsum = [
        remote(msg.at[i, turn2(ic, o)], redz.at[ic, iz], gz.at[0, o, i], gz.at[1, ic, iz], heads=turn(iz, i), dp_2=turn2(ic, o))
        for o in (0, 1) for i in range(4) if o + i > 0
    ]
    over_x = [
        remote(redx.at[ix], redx.at[ix], gx.at[0, i], gx.at[1, i], dp_0=turn(ix, i)) for i in (1, 2, 3)
    ]
    over_y = [
        remote(redy.at[ic, iy], redy.at[ic, iy], gy.at[0, o, i], gy.at[1, ic, iy], dp_1=turn(iy, i), dp_2=turn2(ic, o))
        for o in (0, 1) for i in range(4) if o + i > 0
    ]

    def start(copies):
        for c in copies:
            c.start()

    def finish_copies(copies):
        for c in copies:
            c.wait()

    def last_product(i):
        rows = pl.ds(pl.multiple_of(turn(rank, i) * Q, Q), Q)
        for g in range(G):
            dk = [nt(yt[g, 64 * j : 64 * j + 64, :], p[3 * g + j, rows, :]).astype(BF) for j in range(3)]
            tail = gmid[:, rows] if g == 0 else jnp.zeros((64, Q), BF)
            a[rows, GW * g + 384 : GW * g + GW] = jnp.concatenate(dk + [tail], axis=0).T
        igb[rows, :] = (acc[rows, :] + nn(a[rows, 0 : G * GW], wg[...])).astype(BF)
        if i:
            sent_back(igb, ig_out, isem, i).start()

    @pl.when(owner)
    def _():
        start(zsum)
        redz[ic, iz] = msg[0, ic]
        last_product(2)

    def from_others(buf, sem, c, n, me):
        @pl.when(jnp.logical_or(ic != c, me != n))
        def _():
            pltpu.make_async_copy(redx.at[0], buf.at[c, n], sem.at[1, c, n]).wait()

    total = jnp.zeros((16, 512), F32)
    for c in range(2):
        for z in range(4):
            if (z + 2 * c) % 4 != 3:
                from_others(redz, gz, c, z, iz)
                total = total + redz[c, z].astype(F32)
    redx[ix] = total.astype(BF)
    start(over_x)

    @pl.when(owner)
    def _():
        last_product(1)

    finish_copies(over_x)
    redy[ic, iy] = sum(redx[n].astype(F32) for n in range(4)).astype(BF)
    start(over_y)

    @pl.when(owner)
    def _():
        last_product(3)
        last_product(0)
        own_back(igb, ig_out, isem).start()

    halves = []
    for c in range(2):
        for n in range(4):
            from_others(redy, gy, c, n, iy)
        halves.append(sum(redy[c, n].astype(F32) for n in range(4)))
    gd_out[:, 0:512] = halves[0]
    gd_out[:, 512:768] = halves[1][:, 0:256]
    gu_out[...] = halves[1][:, 256:448]

    back_end(act, act_out, asem)
    back_end(igb, ig_out, isem)
    spread_end(inputs, x, xsem)
    spread_end(cot, ct, csem)
    for c in ups:
        c.wait_send()

    weights_end()

    for c in over_y:
        c.wait_send()

    @pl.when(owner)
    def _():
        for c in zsum:
            c.wait_send()


def finish(act_in, ig_in, gd, gu, act, ig, gdq, guq, gdv, guv):
    act[...] = act_in[...]
    ig[...] = ig_in[...].astype(F32)
    gdq[...] = gd[0:8, :]
    gdv[...] = gd[8:16, :]
    guq[...] = gu[0:8, :]
    guv[...] = gu[8:16, :]


def scratch():
    V, dma = pltpu.VMEM, pltpu.SemaphoreType.DMA
    return [
        V((B, S), jnp.int32), V((D,), F32), V((D,), F32), V((D,), F32), V((D,), F32),
        V((8, D), BF), V((8, 192), BF), V((8, D), BF), V((8, 192), BF),
        V((S, D), BF), V((S, D), BF), V((D, D), BF), V((D, FF), BF), V((FF, D), BF), V((G * GW, D), BF),
        V((G, 16, 384), BF), V((S, D), BF), V((S, D), BF),
        V((64, S), BF), V((64, S), BF), V((G, S, 256), BF), V((G, S, 256), BF), V((G, GW, S), BF),
        V((3, S, 256), F32), V((12, S, S), BF), V((12, 1, S), F32), V((G, 192, S), BF),
        V((S, D), F32), V((S, D), F32), V((S, 1), F32), V((S, D), BF),
        V((2, S, C), F32), V((S, FF), BF), V((S, FF), F32), V((S, D), F32),
        V((G, 192, S), F32), V((3, 64, S), BF), V((G, 384, S), BF),
        V((S, D), BF),
        V((4, 2, 16, 512), BF), V((2, 4, 16, 512), BF), V((4, 16, 512), BF), V((2, 4, 16, 512), BF),
        V((64, S), BF),
        dma((15,)), dma((2, 4)), dma((2, 4)), dma((2, 4)), dma((2, 4)), dma((2, 4, 4)), dma((2, 4, 3, 4)), dma((2, 4)),
        dma((2, 4)), dma((2, 4)), dma((2, 2, 4)), dma((2, 4)), dma((2, 2, 4)),
    ]


def per_device(inputs, key_mask, lengths, cotangent, wq, wk, wv, w_out, w_inner, w_outer, g1, b1, g2, b2, dq, uq, dv, uv):
    vm, hbm = pl.BlockSpec(memory_space=pltpu.VMEM), pl.BlockSpec(memory_space=pl.ANY)
    shape = jax.ShapeDtypeStruct
    act, ig, gd, gu = pl.pallas_call(
        layer,
        out_shape=(shape((B, Q, D), BF), shape((B, Q, D), BF), shape((16, D), F32), shape((16, 192), F32)),
        in_specs=[hbm] * 3 + [pl.BlockSpec(memory_space=pltpu.SMEM)] + [hbm] * 14,
        out_specs=(hbm, hbm, vm, vm),
        scratch_shapes=scratch(),
        compiler_params=pltpu.CompilerParams(
            collective_id=0, has_side_effects=True, vmem_limit_bytes=62 * 2**20
        ),
    )(
        inputs, cotangent, key_mask, lengths, wq.T, wk.T, wv.T, w_out, w_inner, w_outer,
        g1, b1, g2, b2, dq.T, uq, dv.T, uv,
    )
    act, ig, gdq, guq, gdv, guv = pl.pallas_call(
        finish,
        out_shape=(
            shape((B, Q, D), BF), shape((B, Q, D), F32),
            shape((8, D), F32), shape((8, 192), F32), shape((8, D), F32), shape((8, 192), F32),
        ),
        in_specs=[vm] * 4,
        out_specs=(vm,) * 6,
    )(act, ig, gd, gu)
    return act, ig, gdq.T, guq, gdv.T, guv


def solution(mesh):
    finer = Mesh(
        mesh.devices.reshape(4, 4, 2, mesh.shape["heads"]), ("dp_0", "dp_1", "dp_2", "heads")
    )
    rows, cols, same = P(DP, "heads", None), P(None, "heads"), P()
    return jax.shard_map(
        per_device,
        mesh=finer,
        in_specs=(rows, P(DP, None), P(DP), rows, cols, cols, cols) + (same,) * 8 + (cols, same, cols),
        out_specs=(rows, rows, same, cols, same, cols),
        check_vma=False,
    )
```

```python
import functools

import jax
import jax.numpy as jnp
from jax import lax
from jax.experimental import pallas as pl
from jax.experimental.pallas import tpu as pltpu
from jax.sharding import Mesh
from jax.sharding import PartitionSpec as P

BF, F32 = jnp.bfloat16, jnp.float32
S, D, FF, HD, G = 512, 768, 3072, 64, 4
B, Q = 3, 128
GW = 640
C = 512
NT = (((1,), (1,)), ((), ()))
DP = ("dp_0", "dp_1", "dp_2")
MESH = pl.DeviceIdType.MESH


def nn(a, b):
    return jnp.dot(a, b, preferred_element_type=F32)


def nt(a, b):
    return lax.dot_general(a, b, NT, preferred_element_type=F32)


def middle(x, wg, mid):
    mid[0:16, :] = nt(wg[576:592, :], x[...]).astype(BF)
    mid[16:64, :] = jnp.zeros((48, S), BF)


def project(g, x, wg, up, mid, bias, knat, vnat, yt):
    y = nt(wg[GW * g : GW * g + 576, :], x[...])
    upt = jnp.concatenate([up[g], jnp.zeros((112, 384), BF)], axis=0).T
    qv = y[0:384] + nn(upt[:, 0:64], mid[...])
    vt = qv[192:384].astype(BF)
    yt[g, 0:192, :] = (qv[0:192].astype(BF).astype(F32) * 0.125).astype(BF)
    yt[g, 192:384, :] = vt
    vnat[g] = jnp.concatenate([jnp.zeros((64, S), BF), vt], axis=0).T
    kt = jnp.concatenate([y[384:576].astype(BF), bias[...]], axis=0)
    yt[g, 384:GW, :] = kt
    knat[g] = kt.T


def pad_rows(piece, before, total):
    parts, lanes = [], piece.shape[1]
    if before:
        parts.append(jnp.zeros((before, lanes), BF))
    parts.append(piece)
    after = total - before - piece.shape[0]
    if after:
        parts.append(jnp.zeros((after, lanes), BF))
    return jnp.concatenate(parts, axis=0)


def staged(units, *stages):
    for step in range(len(units) + len(stages) - 1):
        for n, stage in enumerate(stages):
            if 0 <= step - n < len(units):
                stage(step - n, *units[step - n])


def half_cols(half):
    return slice(256 * half, 256 * half + 256)


def attend(units, place, knat, yt, sscr, p, rl, ctxt):
    maxima = {}

    def scores(u, g, j, half):
        cols = half_cols(half)
        last = (lax.broadcasted_iota(jnp.int32, (64, 256), 0) == 63).astype(BF)
        rhs = jnp.concatenate([pad_rows(yt[g, 64 * j : 64 * j + 64, cols], 64 * j, 192), last], axis=0)
        s = nn(knat[g], rhs)
        sscr[u % 3] = s
        maxima[u] = jnp.max(s, axis=0, keepdims=True)

    def weights(u, g, j, half):
        p[g * 3 + j, :, half_cols(half)] = jnp.exp(sscr[u % 3] - maxima[u]).astype(BF)

    def mix(u, g, j, half):
        cols = half_cols(half)
        vt = jnp.concatenate([yt[g, 192 + 64 * j : 256 + 64 * j, :], jnp.ones((16, S), BF)], axis=0)
        ot = nn(vt, p[g * 3 + j, :, cols])
        rinv = 1.0 / ot[64:65]
        rl[g * 3 + j, :, cols] = rinv
        ctxt[place(g), 64 * j : 64 * j + 64, cols] = (ot[0:64] * rinv).astype(BF)

    staged(units, scores, weights, mix)


def attend_back(units, place, vnat, yt, p, rl, ctxt, dot_ref, dosc, dyt, group_done):
    def values(u, g, j):
        rows, h = slice(64 * j, 64 * j + 64), g * 3 + j
        do = (dot_ref[place(g), rows, :] * rl[h]).astype(BF)
        dosc[u % 3] = do
        dyt[g, 192 + 64 * j : 256 + 64 * j, :] = nt(do, p[h]).astype(BF)

    def scores(u, g, j):
        rows, h = slice(64 * j, 64 * j + 64), g * 3 + j
        for half in range(2):
            cols = half_cols(half)
            do = dosc[u % 3, :, cols]
            dsum = jnp.sum(do.astype(F32) * ctxt[place(g), rows, cols].astype(F32), axis=0, keepdims=True)
            dp = nn(vnat[g], pad_rows(do, 64 + 64 * j, 256))
            p[h, :, cols] = (p[h, :, cols].astype(F32) * (dp - dsum)).astype(BF)

    def queries(u, g, j):
        ds = p[g * 3 + j]
        dyt[g, 64 * j : 64 * j + 64, :] = (nn(yt[g, 384 + 64 * j : 448 + 64 * j, :], ds) * 0.125).astype(BF)
        if j == 2:
            group_done(g)

    staged(units, values, scores, queries)


def gelu_pair(v):
    e = jnp.exp(v * v * -0.5)
    t = 1.0 / (1.0 + 0.23164189 * jnp.abs(v))
    tail = t * (0.127414796 + t * (-0.142248368 + t * (0.7107068705 + t * (-0.7265760135 + t * 0.5307027145)))) * e
    cdf = jnp.where(v >= 0.0, 1.0 - tail, tail)
    return v * cdf, cdf + v * (e * 0.3989422804)


def norm(h):
    mean = jnp.mean(h, axis=-1, keepdims=True)
    c = h - mean
    r = lax.rsqrt(jnp.mean(c * c, axis=-1, keepdims=True) + 1e-5)
    return c * r, r


def norm_back(n, xhat, r):
    return r * (n - jnp.mean(n, axis=-1, keepdims=True) - xhat * jnp.mean(n * xhat, axis=-1, keepdims=True))


def chunk(c):
    return pl.ds(pl.multiple_of(c * C, C), C)


def feed_forward(n1b, wi, wt, hs, a, dact, acc):
    n = FF // C
    for c in range(n + 2):
        if c < n:
            hs[c % 2] = nn(n1b[...], wi[:, C * c : C * c + C])
        if 0 < c <= n:
            cols = slice(C * (c - 1), C * c)
            v, d = gelu_pair(hs[(c - 1) % 2])
            a[:, cols] = v.astype(BF)
            dact[:, cols] = d
        if c > 1:
            cols = slice(C * (c - 2), C * (c - 1))
            acc[...] += nn(a[:, cols], wt[cols, :])


def feed_back(gnb, wi, wt, a, dact, acc):
    for c in range(FF // C):
        cols = slice(C * c, C * c + C)
        a[:, cols] = (nt(gnb[...], wt[cols, :]) * dact[:, cols]).astype(BF)
    acc[...] += nt(a[...], wi[...])
NEAR = (1, 3, 2)


def remote(src, dst, send, recv, **where):
    return pltpu.make_async_remote_copy(
        src_ref=src, dst_ref=dst, send_sem=send, recv_sem=recv, device_id=where, device_id_type=MESH
    )


def layer(
    inputs, cot, kmask_in, lengths, wq, wk, wv, w_out, w_inner, w_outer, g1_in, b1_in, g2_in, b2_in, dq_in, uq_in, dv_in, uv_in,
    act_out, ig_out, gd_out, gu_out,
    kmask, g1, b1, g2, b2, dq, uq, dv, uv, x, ct, wo, wi, wt, wg, up, act, igb,
    bias, mid, knat, vnat, yt, sscr, p, rl, ctxt, xhat1, xhat2, r1s, n1b, hs, a, dact, acc,
    dot_ref, dosc, dyt, gnb,
    msg, redz, redx, redy, gmid,
    lsem, xsem, csem, wsem, usem, w1, w2, w3, asem, isem, gz, gx, gy,
):
    ix, iy, ic, iz = (lax.axis_index(n) for n in ("dp_0", "dp_1", "dp_2", "heads"))
    rank = lax.rem(iz + 2 * ic, 4)
    owner = rank < 3
    mine = jnp.minimum(rank, 2)

    def z_of(r):
        return lax.rem(r + 2 * ic, 4)

    def turn(i, by):
        return lax.rem(i + by, 4)

    def turn2(i, by):
        return lax.rem(i + by, 2)

    def place(g):
        return turn(iz, g)

    barrier = pltpu.get_barrier_semaphore()
    peers = [{"dp_2": 1 - ic}]
    for i in (1, 2, 3):
        peers += [{"heads": turn(iz, i)}, {"dp_0": turn(ix, i)}, {"dp_1": turn(iy, i)}]
    for i in (1, 2, 3):
        peers += [{"heads": turn(iz, i), "dp_2": 1 - ic}, {"dp_1": turn(iy, i), "dp_2": 1 - ic}]
    for where in peers:
        pl.semaphore_signal(barrier, inc=1, device_id=where, device_id_type=MESH)
    weights = (wq, wv, wk)
    loads = [pltpu.make_async_copy(w, wg.at[pl.ds(192 * n, 192)], lsem.at[n]) for n, w in enumerate(weights)]
    late = [
        pltpu.make_async_copy(w, v, lsem.at[3 + n]) for n, (w, v) in enumerate(((w_out, wo), (w_inner, wi), (w_outer, wt)))
    ]
    small = [
        pltpu.make_async_copy(src, dst, lsem.at[6 + n])
        for n, (src, dst) in enumerate(
            ((kmask_in, kmask), (g1_in, g1), (b1_in, b1), (g2_in, g2), (b2_in, b2),
             (dq_in, dq), (uq_in, uq), (dv_in, dv), (uv_in, uv))
        )
    ]
    for c in loads + small:
        c.start()
    pl.semaphore_wait(barrier, 16)
    for c in loads:
        c.wait()

    la, lb = ix * (1 - ic) + iy * ic, iy * (1 - ic) + ix * ic
    holds = la < 3

    def part(k, at, count, core=ic):
        rows = pl.ds(pl.multiple_of(GW * k + at, 16), count)
        return wg.at[rows, pl.ds(pl.multiple_of(384 * core, 128), 384)]

    def piece(k, a):
        return part(k, 48 * (3 * lb + a), 48)

    def along_a(i):
        return {"dp_0": turn(ix, i * (1 - ic)), "dp_1": turn(iy, i * ic)}

    def along_b(i):
        return {"dp_0": turn(ix, i * ic), "dp_1": turn(iy, i * (1 - ic))}

    def over_z(i):
        return remote(piece(0, la), piece(4 - i, la), wsem.at[0, i], wsem.at[1, 4 - i], heads=turn(iz, i))

    def first(k, i):
        return remote(piece(k, la), piece(k, la), w1.at[0, k, i], w1.at[1, k, i], **along_a(i))

    def second(k, a, i):
        return remote(piece(k, a), piece(k, a), w2.at[0, k, a, i], w2.at[1, k, a, i], **along_b(i))

    def third(k, core=ic):
        what = part(k, 0, 576, core)
        return remote(what, what, w3.at[0, k], w3.at[1, k], dp_2=1 - ic)

    def join_line():
        @pl.when(holds)
        def _():
            for k in NEAR:
                over_z(4 - k).wait_recv()
                for i in NEAR:
                    first(k, i).start()
                for i in NEAR:
                    second(k, la, i).start()

        for k in NEAR:
            for i in NEAR:
                source = turn(la, 4 - i)

                @pl.when(source < 3)
                def _():
                    first(k, i).wait_recv()
                    for n in NEAR:
                        second(k, source, n).start()

    def join(k):
        for a in range(3):
            for i in (1, 2, 3):
                second(k, a, i).wait_recv()
        third(k).start()

    def arrived(k):
        third(k, 1 - ic).wait_recv()

    def weights_end():
        @pl.when(holds)
        def _():
            for i in (1, 2, 3):
                over_z(i).wait_send()
                for k in (1, 2, 3):
                    first(k, i).wait_send()

        for k in (1, 2, 3):
            for a in range(3):
                for i in (1, 2, 3):
                    second(k, a, i).wait_send()
            third(k).wait_send()

    @pl.when(holds)
    def _():
        for i in (1, 3, 2):
            over_z(i).start()

    def slot(ref, r):
        return ref.at[pl.ds(pl.multiple_of(r * Q, Q), Q)]

    def spread_to(src, dst, sem, i):
        j = jnp.minimum(turn(rank, i), 2)
        return remote(src.at[j], slot(dst, rank), sem.at[0, i], sem.at[1, rank], heads=turn(iz, i))

    def spread(src, dst, sem):
        for i in (2, 1, 3):
            pl.when(turn(rank, i) < 3)(spread_to(src, dst, sem, i).start)

        @pl.when(owner)
        def _():
            pltpu.make_async_copy(src.at[mine], slot(dst, mine), sem.at[1, mine]).start()

    def spread_wait(src, dst, sem):
        @pl.when(owner)
        def _():
            for r in range(4):
                pltpu.make_async_copy(src.at[0], dst.at[pl.ds(r * Q, Q)], sem.at[1, r]).wait()

    def spread_end(src, dst, sem):
        for i in (1, 2, 3):
            pl.when(turn(rank, i) < 3)(spread_to(src, dst, sem, i).wait_send)

    spread(inputs, x, xsem)

    for c in small:
        c.wait()
    zero8 = jnp.zeros((8, 192), F32)
    both = jnp.concatenate(
        [
            jnp.concatenate([uq[...].astype(F32), zero8], axis=1),
            jnp.concatenate([zero8, uv[...].astype(F32)], axis=1),
        ],
        axis=0,
    )
    up[0] = (2.0 * both).astype(BF)
    ups = [
        remote(up.at[0], up.at[4 - i], usem.at[0, i], usem.at[1, 4 - i], heads=turn(iz, i)) for i in (1, 2, 3)
    ]
    for c in ups:
        c.start()
    down = jnp.concatenate([dq[...].astype(F32), dv[...].astype(F32)], axis=0).astype(BF)
    for g in range(G):
        wg[GW * g + 576 : GW * g + GW, :] = jnp.concatenate(
            [down if g == 0 else jnp.zeros((16, D), BF), jnp.zeros((48, D), BF)], axis=0
        )

    join_line()
    for c in late:
        c.start()

    row = jnp.where(mine == 0, kmask[0:1], jnp.where(mine == 1, kmask[1:2], kmask[2:3]))
    row = jnp.where(ic == 0, row, jnp.concatenate([row[:, 256:512], row[:, 0:256]], axis=1))
    row = jnp.where(row > 0, 0.0, -1e30).astype(F32)
    bias[...] = jnp.where(lax.broadcasted_iota(jnp.int32, (64, S), 0) == 63, row, 0.0).astype(BF)
    for c in ups:
        c.wait_recv()
    spread_wait(inputs, x, xsem)
    spread_end(inputs, x, xsem)
    spread(cot, ct, csem)

    def project_group(g):
        project(g, x, wg, up, mid, bias, knat, vnat, yt)

    def attend_some(units):
        attend(units, place, knat, yt, sscr, p, rl, ctxt)

    def all_of(g):
        return [(g, j, half) for half in (1, 0) for j in range(3)]

    order = (0,) + NEAR

    @pl.when(owner)
    def _():
        middle(x, wg, mid)
        project_group(0)

    join(order[1])

    @pl.when(owner)
    def _():
        attend_some(all_of(0))

    for n in range(3):
        if n < 2:
            join(order[n + 2])
        arrived(order[n + 1])

        @pl.when(owner)
        def _():
            project_group(order[n + 1])
            attend_some(all_of(order[n + 1]))

    for c in late:
        c.wait()

    def rows_of(src, t):
        return src.at[pl.ds(pl.multiple_of(t * Q, Q), Q)]

    def sent_back(src, dst, sem, i):
        return remote(rows_of(src, turn(rank, i)), dst.at[mine], sem.at[0, i], sem.at[1, mine], heads=turn(iz, i))

    def own_back(src, dst, sem):
        return pltpu.make_async_copy(rows_of(src, mine), dst.at[mine], sem.at[1, mine])

    def back(src, dst, sem):
        for i in (1, 2, 3):
            sent_back(src, dst, sem, i).start()
        own_back(src, dst, sem).start()

    def back_end(src, dst, sem):
        for j in range(B):
            pltpu.make_async_copy(src.at[pl.ds(0, Q)], dst.at[j], sem.at[1, j]).wait()

        @pl.when(owner)
        def _():
            for i in (1, 2, 3):
                sent_back(src, dst, sem, i).wait_send()

    @pl.when(owner)
    def _():
        ctx = jnp.concatenate([ctxt[g].T for g in range(G)], axis=1)
        xh, r = norm(x[...].astype(F32) + nn(ctx, wo[...]))
        xhat1[...] = xh
        r1s[...] = r
        n1v = xh * g1[...][None] + b1[...][None]
        n1b[...] = n1v.astype(BF)
        acc[...] = n1v
        feed_forward(n1b, wi, wt, hs, a, dact, acc)
        xh2, r2 = norm(acc[...])
        act[...] = (xh2 * g2[...][None] + b2[...][None]).astype(BF)
        xhat2[...] = xh2
        back(act, act_out, asem)
        acc[:, 0:1] = r2

    spread_wait(cot, ct, csem)

    @pl.when(owner)
    def _():
        limit = lengths[mine]
        at = lax.broadcasted_iota(jnp.int32, (Q, 1), 0)
        valid = jnp.concatenate([at + z_of(t) * Q < limit for t in range(4)], axis=0)
        tangent = jnp.where(valid, ct[...].astype(F32), 0.0)
        gs = norm_back(tangent * g2[...][None], xhat2[...], acc[:, 0:1])
        gnb[...] = gs.astype(BF)
        acc[...] = gs
        feed_back(gnb, wi, wt, a, dact, acc)
        gf1 = norm_back(acc[...] * g1[...][None], xhat1[...], r1s[...])
        acc[...] = gf1
        gfb = gf1.astype(BF)
        for g in range(G):
            dot_ref[g] = nt(wo[192 * g : 192 * g + 192, :], gfb)
        middle_sum = [jnp.zeros((16, S), F32)]
        first_rows = lax.broadcasted_iota(jnp.int32, (16, 192), 0) < 8

        def group_done(g):
            dqv = dyt[g]
            a[:, GW * g : GW * g + 384] = dqv.T
            gu = nt(mid[0:16, :], dqv)
            gu = jnp.where(first_rows, gu[:, 0:192], gu[:, 192:384]) * 2.0
            msg[g, 1, :, 256:512] = jnp.concatenate([gu, jnp.zeros((16, 64), F32)], axis=1).astype(BF)
            middle_sum[0] = middle_sum[0] + nn(up[g], dqv)

        attend_back([(g, j) for g in range(G) for j in range(3)], place, vnat, yt, p, rl, ctxt, dot_ref, dosc, dyt, group_done)
        gmb = middle_sum[0].astype(BF)
        gmid[0:16, :] = gmb
        gmid[16:64, :] = jnp.zeros((48, S), BF)
        gd = nn(gmb, x[...]).astype(BF)
        for g in range(G):
            msg[g, 0] = gd[:, 0:512]
            msg[g, 1, :, 0:256] = gd[:, 512:768]

    zsum = [
        remote(msg.at[i, turn2(ic, o)], redz.at[ic, iz], gz.at[0, o, i], gz.at[1, ic, iz], heads=turn(iz, i), dp_2=turn2(ic, o))
        for o in (0, 1) for i in range(4) if o + i > 0
    ]
    over_x = [
        remote(redx.at[ix], redx.at[ix], gx.at[0, i], gx.at[1, i], dp_0=turn(ix, i)) for i in (1, 2, 3)
    ]
    over_y = [
        remote(redy.at[ic, iy], redy.at[ic, iy], gy.at[0, o, i], gy.at[1, ic, iy], dp_1=turn(iy, i), dp_2=turn2(ic, o))
        for o in (0, 1) for i in range(4) if o + i > 0
    ]

    def start(copies):
        for c in copies:
            c.start()

    def finish_copies(copies):
        for c in copies:
            c.wait()

    def last_product(i):
        rows = pl.ds(pl.multiple_of(turn(rank, i) * Q, Q), Q)
        for g in range(G):
            dk = [nt(yt[g, 64 * j : 64 * j + 64, :], p[3 * g + j, rows, :]).astype(BF) for j in range(3)]
            tail = gmid[:, rows] if g == 0 else jnp.zeros((64, Q), BF)
            a[rows, GW * g + 384 : GW * g + GW] = jnp.concatenate(dk + [tail], axis=0).T
        igb[rows, :] = (acc[rows, :] + nn(a[rows, 0 : G * GW], wg[...])).astype(BF)
        if i:
            sent_back(igb, ig_out, isem, i).start()

    @pl.when(owner)
    def _():
        start(zsum)
        redz[ic, iz] = msg[0, ic]
        last_product(2)
        last_product(1)

    def from_others(buf, sem, c, n, me):
        @pl.when(jnp.logical_or(ic != c, me != n))
        def _():
            pltpu.make_async_copy(redx.at[0], buf.at[c, n], sem.at[1, c, n]).wait()

    total = jnp.zeros((16, 512), F32)
    for c in range(2):
        for z in range(4):
            if (z + 2 * c) % 4 != 3:
                from_others(redz, gz, c, z, iz)
                total = total + redz[c, z].astype(F32)
    redx[ix] = total.astype(BF)
    start(over_x)

    @pl.when(owner)
    def _():
        last_product(3)

    finish_copies(over_x)
    redy[ic, iy] = sum(redx[n].astype(F32) for n in range(4)).astype(BF)
    start(over_y)

    @pl.when(owner)
    def _():
        last_product(0)
        own_back(igb, ig_out, isem).start()

    halves = []
    for c in range(2):
        for n in range(4):
            from_others(redy, gy, c, n, iy)
        halves.append(sum(redy[c, n].astype(F32) for n in range(4)))
    gd_out[:, 0:512] = halves[0]
    gd_out[:, 512:768] = halves[1][:, 0:256]
    gu_out[...] = halves[1][:, 256:448]

    back_end(act, act_out, asem)
    back_end(igb, ig_out, isem)
    spread_end(cot, ct, csem)
    for c in ups:
        c.wait_send()

    weights_end()

    for c in over_y:
        c.wait_send()

    @pl.when(owner)
    def _():
        for c in zsum:
            c.wait_send()


def finish(act_in, ig_in, gd, gu, act, ig, gdq, guq, gdv, guv):
    act[...] = act_in[...]
    ig[...] = ig_in[...].astype(F32)
    gdq[...] = gd[0:8, :]
    gdv[...] = gd[8:16, :]
    guq[...] = gu[0:8, :]
    guv[...] = gu[8:16, :]


def scratch():
    V, dma = pltpu.VMEM, pltpu.SemaphoreType.DMA
    return [
        V((B, S), jnp.int32), V((D,), F32), V((D,), F32), V((D,), F32), V((D,), F32),
        V((8, D), BF), V((8, 192), BF), V((8, D), BF), V((8, 192), BF),
        V((S, D), BF), V((S, D), BF), V((D, D), BF), V((D, FF), BF), V((FF, D), BF), V((G * GW, D), BF),
        V((G, 16, 384), BF), V((S, D), BF), V((S, D), BF),
        V((64, S), BF), V((64, S), BF), V((G, S, 256), BF), V((G, S, 256), BF), V((G, GW, S), BF),
        V((3, S, 256), F32), V((12, S, S), BF), V((12, 1, S), F32), V((G, 192, S), BF),
        V((S, D), F32), V((S, D), F32), V((S, 1), F32), V((S, D), BF),
        V((2, S, C), F32), V((S, FF), BF), V((S, FF), F32), V((S, D), F32),
        V((G, 192, S), F32), V((3, 64, S), BF), V((G, 384, S), BF),
        V((S, D), BF),
        V((4, 2, 16, 512), BF), V((2, 4, 16, 512), BF), V((4, 16, 512), BF), V((2, 4, 16, 512), BF),
        V((64, S), BF),
        dma((15,)), dma((2, 4)), dma((2, 4)), dma((2, 4)), dma((2, 4)), dma((2, 4, 4)), dma((2, 4, 3, 4)), dma((2, 4)),
        dma((2, 4)), dma((2, 4)), dma((2, 2, 4)), dma((2, 4)), dma((2, 2, 4)),
    ]


def per_device(inputs, key_mask, lengths, cotangent, wq, wk, wv, w_out, w_inner, w_outer, g1, b1, g2, b2, dq, uq, dv, uv):
    vm, hbm = pl.BlockSpec(memory_space=pltpu.VMEM), pl.BlockSpec(memory_space=pl.ANY)
    shape = jax.ShapeDtypeStruct
    act, ig, gd, gu = pl.pallas_call(
        layer,
        out_shape=(shape((B, Q, D), BF), shape((B, Q, D), BF), shape((16, D), F32), shape((16, 192), F32)),
        in_specs=[hbm] * 3 + [pl.BlockSpec(memory_space=pltpu.SMEM)] + [hbm] * 14,
        out_specs=(hbm, hbm, vm, vm),
        scratch_shapes=scratch(),
        compiler_params=pltpu.CompilerParams(
            collective_id=0, has_side_effects=True, vmem_limit_bytes=62 * 2**20
        ),
    )(
        inputs, cotangent, key_mask, lengths, wq.T, wk.T, wv.T, w_out, w_inner, w_outer,
        g1, b1, g2, b2, dq.T, uq, dv.T, uv,
    )
    act, ig, gdq, guq, gdv, guv = pl.pallas_call(
        finish,
        out_shape=(
            shape((B, Q, D), BF), shape((B, Q, D), F32),
            shape((8, D), F32), shape((8, 192), F32), shape((8, D), F32), shape((8, 192), F32),
        ),
        in_specs=[vm] * 4,
        out_specs=(vm,) * 6,
    )(act, ig, gd, gu)
    return act, ig, gdq.T, guq, gdv.T, guv


def solution(mesh):
    finer = Mesh(
        mesh.devices.reshape(4, 4, 2, mesh.shape["heads"]), ("dp_0", "dp_1", "dp_2", "heads")
    )
    rows, cols, same = P(DP, "heads", None), P(None, "heads"), P()
    return jax.shard_map(
        per_device,
        mesh=finer,
        in_specs=(rows, P(DP, None), P(DP), rows, cols, cols, cols) + (same,) * 8 + (cols, same, cols),
        out_specs=(rows, rows, same, cols, same, cols),
        check_vma=False,
    )
```

```python
import functools

import jax
import jax.numpy as jnp
from jax import lax
from jax.experimental import pallas as pl
from jax.experimental.pallas import tpu as pltpu
from jax.sharding import Mesh
from jax.sharding import PartitionSpec as P

BF, F32 = jnp.bfloat16, jnp.float32
S, D, FF, HD, G = 512, 768, 3072, 64, 4
B, Q = 3, 128
GW = 640
C = 512
NT = (((1,), (1,)), ((), ()))
DP = ("dp_0", "dp_1", "dp_2")
MESH = pl.DeviceIdType.MESH


def nn(a, b):
    return jnp.dot(a, b, preferred_element_type=F32)


def nt(a, b):
    return lax.dot_general(a, b, NT, preferred_element_type=F32)


def middle(x, wg, mid):
    mid[0:16, :] = nt(wg[576:592, :], x[...]).astype(BF)
    mid[16:64, :] = jnp.zeros((48, S), BF)


def project(g, x, wg, up, mid, bias, knat, vnat, yt):
    y = nt(wg[GW * g : GW * g + 576, :], x[...])
    upt = jnp.concatenate([up[g], jnp.zeros((112, 384), BF)], axis=0).T
    qv = y[0:384] + nn(upt[:, 0:64], mid[...])
    vt = qv[192:384].astype(BF)
    yt[g, 0:192, :] = (qv[0:192].astype(BF).astype(F32) * 0.125).astype(BF)
    yt[g, 192:384, :] = vt
    vnat[g] = jnp.concatenate([jnp.zeros((64, S), BF), vt], axis=0).T
    kt = jnp.concatenate([y[384:576].astype(BF), bias[...]], axis=0)
    yt[g, 384:GW, :] = kt
    knat[g] = kt.T


def pad_rows(piece, before, total):
    parts, lanes = [], piece.shape[1]
    if before:
        parts.append(jnp.zeros((before, lanes), BF))
    parts.append(piece)
    after = total - before - piece.shape[0]
    if after:
        parts.append(jnp.zeros((after, lanes), BF))
    return jnp.concatenate(parts, axis=0)


def staged(units, *stages):
    for step in range(len(units) + len(stages) - 1):
        for n, stage in enumerate(stages):
            if 0 <= step - n < len(units):
                stage(step - n, *units[step - n])


def half_cols(half):
    return slice(256 * half, 256 * half + 256)


def attend(units, place, knat, yt, sscr, p, rl, ctxt):
    maxima = {}

    def scores(u, g, j, half):
        cols = half_cols(half)
        last = (lax.broadcasted_iota(jnp.int32, (64, 256), 0) == 63).astype(BF)
        rhs = jnp.concatenate([pad_rows(yt[g, 64 * j : 64 * j + 64, cols], 64 * j, 192), last], axis=0)
        s = nn(knat[g], rhs)
        sscr[u % 3] = s
        maxima[u] = jnp.max(s, axis=0, keepdims=True)

    def weights(u, g, j, half):
        p[g * 3 + j, :, half_cols(half)] = jnp.exp(sscr[u % 3] - maxima[u]).astype(BF)

    def mix(u, g, j, half):
        cols = half_cols(half)
        vt = jnp.concatenate([yt[g, 192 + 64 * j : 256 + 64 * j, :], jnp.ones((16, S), BF)], axis=0)
        ot = nn(vt, p[g * 3 + j, :, cols])
        rinv = 1.0 / ot[64:65]
        rl[g * 3 + j, :, cols] = rinv
        ctxt[place(g), 64 * j : 64 * j + 64, cols] = (ot[0:64] * rinv).astype(BF)

    staged(units, scores, weights, mix)


def attend_back(units, place, vnat, yt, p, rl, ctxt, dot_ref, dosc, dyt, group_done):
    def values(u, g, j):
        rows, h = slice(64 * j, 64 * j + 64), g * 3 + j
        do = (dot_ref[place(g), rows, :] * rl[h]).astype(BF)
        dosc[u % 3] = do
        dyt[g, 192 + 64 * j : 256 + 64 * j, :] = nt(do, p[h]).astype(BF)

    def scores(u, g, j):
        rows, h = slice(64 * j, 64 * j + 64), g * 3 + j
        for half in range(2):
            cols = half_cols(half)
            do = dosc[u % 3, :, cols]
            dsum = jnp.sum(do.astype(F32) * ctxt[place(g), rows, cols].astype(F32), axis=0, keepdims=True)
            dp = nn(vnat[g], pad_rows(do, 64 + 64 * j, 256))
            p[h, :, cols] = (p[h, :, cols].astype(F32) * (dp - dsum)).astype(BF)

    def queries(u, g, j):
        ds = p[g * 3 + j]
        dyt[g, 64 * j : 64 * j + 64, :] = (nn(yt[g, 384 + 64 * j : 448 + 64 * j, :], ds) * 0.125).astype(BF)
        if j == 2:
            group_done(g)

    staged(units, values, scores, queries)


def gelu_pair(v):
    e = jnp.exp2(v * (v * -0.7213475204444817))
    t = 1.0 / (1.0 + 0.23164189 * jnp.abs(v))
    tail = t * (0.127414796 + t * (-0.142248368 + t * (0.7107068705 + t * (-0.7265760135 + t * 0.5307027145)))) * e
    cdf = jnp.where(v >= 0.0, 1.0 - tail, tail)
    return v * cdf, cdf + v * (e * 0.3989422804)


def norm(h):
    mean = jnp.mean(h, axis=-1, keepdims=True)
    c = h - mean
    r = lax.rsqrt(jnp.mean(c * c, axis=-1, keepdims=True) + 1e-5)
    return c * r, r


def norm_back(n, xhat, r):
    return r * (n - jnp.mean(n, axis=-1, keepdims=True) - xhat * jnp.mean(n * xhat, axis=-1, keepdims=True))


def chunk(c):
    return pl.ds(pl.multiple_of(c * C, C), C)


def feed_forward(n1b, wi, wt, hs, a, dact, acc):
    n = FF // C
    for c in range(n + 2):
        if c < n:
            hs[c % 2] = nn(n1b[...], wi[:, C * c : C * c + C])
        if 0 < c <= n:
            cols = slice(C * (c - 1), C * c)
            v, d = gelu_pair(hs[(c - 1) % 2])
            a[:, cols] = v.astype(BF)
            dact[:, cols] = d
        if c > 1:
            cols = slice(C * (c - 2), C * (c - 1))
            acc[...] += nn(a[:, cols], wt[cols, :])


def feed_back(gnb, wi, wt, a, dact, acc):
    for c in range(FF // C):
        cols = slice(C * c, C * c + C)
        a[:, cols] = (nt(gnb[...], wt[cols, :]) * dact[:, cols]).astype(BF)
    acc[...] += nt(a[...], wi[...])
NEAR = (1, 3, 2)


def remote(src, dst, send, recv, **where):
    return pltpu.make_async_remote_copy(
        src_ref=src, dst_ref=dst, send_sem=send, recv_sem=recv, device_id=where, device_id_type=MESH
    )


def layer(
    inputs, cot, kmask_in, lengths, wq, wk, wv, w_out, w_inner, w_outer, g1_in, b1_in, g2_in, b2_in, dq_in, uq_in, dv_in, uv_in,
    act_out, ig_out, gd_out, gu_out,
    kmask, g1, b1, g2, b2, dq, uq, dv, uv, x, ct, wo, wi, wt, wg, up, act, igb,
    bias, mid, knat, vnat, yt, sscr, p, rl, ctxt, xhat1, xhat2, r1s, n1b, hs, a, dact, acc,
    dot_ref, dosc, dyt, gnb,
    msg, redz, redx, redy, gmid,
    lsem, xsem, csem, wsem, usem, w1, w2, w3, asem, isem, gz, gx, gy,
):
    ix, iy, ic, iz = (lax.axis_index(n) for n in ("dp_0", "dp_1", "dp_2", "heads"))
    rank = lax.rem(iz + 2 * ic, 4)
    owner = rank < 3
    mine = jnp.minimum(rank, 2)

    def z_of(r):
        return lax.rem(r + 2 * ic, 4)

    def turn(i, by):
        return lax.rem(i + by, 4)

    def turn2(i, by):
        return lax.rem(i + by, 2)

    def place(g):
        return turn(iz, g)

    barrier = pltpu.get_barrier_semaphore()
    peers = [{"dp_2": 1 - ic}]
    for i in (1, 2, 3):
        peers += [{"heads": turn(iz, i)}, {"dp_0": turn(ix, i)}, {"dp_1": turn(iy, i)}]
    for i in (1, 2, 3):
        peers += [{"heads": turn(iz, i), "dp_2": 1 - ic}, {"dp_1": turn(iy, i), "dp_2": 1 - ic}]
    for where in peers:
        pl.semaphore_signal(barrier, inc=1, device_id=where, device_id_type=MESH)
    weights = (wq, wv, wk)
    loads = [pltpu.make_async_copy(w, wg.at[pl.ds(192 * n, 192)], lsem.at[n]) for n, w in enumerate(weights)]
    late = [
        pltpu.make_async_copy(w, v, lsem.at[3 + n]) for n, (w, v) in enumerate(((w_out, wo), (w_inner, wi), (w_outer, wt)))
    ]
    small = [
        pltpu.make_async_copy(src, dst, lsem.at[6 + n])
        for n, (src, dst) in enumerate(
            ((kmask_in, kmask), (g1_in, g1), (b1_in, b1), (g2_in, g2), (b2_in, b2),
             (dq_in, dq), (uq_in, uq), (dv_in, dv), (uv_in, uv))
        )
    ]
    for c in loads + small:
        c.start()
    pl.semaphore_wait(barrier, 16)
    for c in loads:
        c.wait()

    la, lb = ix * (1 - ic) + iy * ic, iy * (1 - ic) + ix * ic
    holds = la < 3

    def part(k, at, count, core=ic):
        rows = pl.ds(pl.multiple_of(GW * k + at, 16), count)
        return wg.at[rows, pl.ds(pl.multiple_of(384 * core, 128), 384)]

    def piece(k, a):
        return part(k, 48 * (3 * lb + a), 48)

    def along_a(i):
        return {"dp_0": turn(ix, i * (1 - ic)), "dp_1": turn(iy, i * ic)}

    def along_b(i):
        return {"dp_0": turn(ix, i * ic), "dp_1": turn(iy, i * (1 - ic))}

    def over_z(i):
        return remote(piece(0, la), piece(4 - i, la), wsem.at[0, i], wsem.at[1, 4 - i], heads=turn(iz, i))

    def first(k, i):
        return remote(piece(k, la), piece(k, la), w1.at[0, k, i], w1.at[1, k, i], **along_a(i))

    def second(k, a, i):
        return remote(piece(k, a), piece(k, a), w2.at[0, k, a, i], w2.at[1, k, a, i], **along_b(i))

    def third(k, core=ic):
        what = part(k, 0, 576, core)
        return remote(what, what, w3.at[0, k], w3.at[1, k], dp_2=1 - ic)

    def join_line():
        @pl.when(holds)
        def _():
            for k in NEAR:
                over_z(4 - k).wait_recv()
                for i in NEAR:
                    first(k, i).start()
                for i in NEAR:
                    second(k, la, i).start()

        for k in NEAR:
            for i in NEAR:
                source = turn(la, 4 - i)

                @pl.when(source < 3)
                def _():
                    first(k, i).wait_recv()
                    for n in NEAR:
                        second(k, source, n).start()

    def join(k):
        for a in range(3):
            for i in (1, 2, 3):
                second(k, a, i).wait_recv()
        third(k).start()

    def arrived(k):
        third(k, 1 - ic).wait_recv()

    def weights_end():
        @pl.when(holds)
        def _():
            for i in (1, 2, 3):
                over_z(i).wait_send()
                for k in (1, 2, 3):
                    first(k, i).wait_send()

        for k in (1, 2, 3):
            for a in range(3):
                for i in (1, 2, 3):
                    second(k, a, i).wait_send()
            third(k).wait_send()

    @pl.when(holds)
    def _():
        for i in (1, 3, 2):
            over_z(i).start()

    def slot(ref, r):
        return ref.at[pl.ds(pl.multiple_of(r * Q, Q), Q)]

    def spread_to(src, dst, sem, i):
        j = jnp.minimum(turn(rank, i), 2)
        return remote(src.at[j], slot(dst, rank), sem.at[0, i], sem.at[1, rank], heads=turn(iz, i))

    def spread(src, dst, sem):
        for i in (2, 1, 3):
            pl.when(turn(rank, i) < 3)(spread_to(src, dst, sem, i).start)

        @pl.when(owner)
        def _():
            pltpu.make_async_copy(src.at[mine], slot(dst, mine), sem.at[1, mine]).start()

    def spread_wait(src, dst, sem):
        @pl.when(owner)
        def _():
            for r in range(4):
                pltpu.make_async_copy(src.at[0], dst.at[pl.ds(r * Q, Q)], sem.at[1, r]).wait()

    def spread_end(src, dst, sem):
        for i in (1, 2, 3):
            pl.when(turn(rank, i) < 3)(spread_to(src, dst, sem, i).wait_send)

    spread(inputs, x, xsem)

    for c in small:
        c.wait()
    zero8 = jnp.zeros((8, 192), F32)
    both = jnp.concatenate(
        [
            jnp.concatenate([uq[...].astype(F32), zero8], axis=1),
            jnp.concatenate([zero8, uv[...].astype(F32)], axis=1),
        ],
        axis=0,
    )
    up[0] = (2.0 * both).astype(BF)
    ups = [
        remote(up.at[0], up.at[4 - i], usem.at[0, i], usem.at[1, 4 - i], heads=turn(iz, i)) for i in (1, 2, 3)
    ]
    for c in ups:
        c.start()
    down = jnp.concatenate([dq[...].astype(F32), dv[...].astype(F32)], axis=0).astype(BF)
    for g in range(G):
        wg[GW * g + 576 : GW * g + GW, :] = jnp.concatenate(
            [down if g == 0 else jnp.zeros((16, D), BF), jnp.zeros((48, D), BF)], axis=0
        )

    join_line()

    row = jnp.where(mine == 0, kmask[0:1], jnp.where(mine == 1, kmask[1:2], kmask[2:3]))
    row = jnp.where(ic == 0, row, jnp.concatenate([row[:, 256:512], row[:, 0:256]], axis=1))
    row = jnp.where(row > 0, 0.0, -1e30).astype(F32)
    bias[...] = jnp.where(lax.broadcasted_iota(jnp.int32, (64, S), 0) == 63, row, 0.0).astype(BF)
    for c in ups:
        c.wait_recv()
    spread_wait(inputs, x, xsem)

    def project_group(g):
        project(g, x, wg, up, mid, bias, knat, vnat, yt)

    def attend_some(units):
        attend(units, place, knat, yt, sscr, p, rl, ctxt)

    def all_of(g):
        return [(g, j, half) for half in (1, 0) for j in range(3)]

    order = (0,) + NEAR

    @pl.when(owner)
    def _():
        middle(x, wg, mid)
        project_group(0)

    spread_end(inputs, x, xsem)
    spread(cot, ct, csem)
    for c in late:
        c.start()
    join(order[1])

    @pl.when(owner)
    def _():
        attend_some(all_of(0))

    for n in range(3):
        if n < 2:
            join(order[n + 2])
        arrived(order[n + 1])

        @pl.when(owner)
        def _():
            project_group(order[n + 1])
            attend_some(all_of(order[n + 1]))

    for c in late:
        c.wait()

    def rows_of(src, t):
        return src.at[pl.ds(pl.multiple_of(t * Q, Q), Q)]

    def sent_back(src, dst, sem, i):
        return remote(rows_of(src, turn(rank, i)), dst.at[mine], sem.at[0, i], sem.at[1, mine], heads=turn(iz, i))

    def own_back(src, dst, sem):
        return pltpu.make_async_copy(rows_of(src, mine), dst.at[mine], sem.at[1, mine])

    def back(src, dst, sem):
        for i in (1, 2, 3):
            sent_back(src, dst, sem, i).start()
        own_back(src, dst, sem).start()

    def back_end(src, dst, sem):
        for j in range(B):
            pltpu.make_async_copy(src.at[pl.ds(0, Q)], dst.at[j], sem.at[1, j]).wait()

        @pl.when(owner)
        def _():
            for i in (1, 2, 3):
                sent_back(src, dst, sem, i).wait_send()

    @pl.when(owner)
    def _():
        ctx = jnp.concatenate([ctxt[g].T for g in range(G)], axis=1)
        xh, r = norm(x[...].astype(F32) + nn(ctx, wo[...]))
        xhat1[...] = xh
        r1s[...] = r
        n1v = xh * g1[...][None] + b1[...][None]
        n1b[...] = n1v.astype(BF)
        acc[...] = n1v
        feed_forward(n1b, wi, wt, hs, a, dact, acc)
        xh2, r2 = norm(acc[...])
        act[...] = (xh2 * g2[...][None] + b2[...][None]).astype(BF)
        xhat2[...] = xh2
        back(act, act_out, asem)
        acc[:, 0:1] = r2

    spread_wait(cot, ct, csem)

    @pl.when(owner)
    def _():
        limit = lengths[mine]
        at = lax.broadcasted_iota(jnp.int32, (Q, 1), 0)
        valid = jnp.concatenate([at + z_of(t) * Q < limit for t in range(4)], axis=0)
        tangent = jnp.where(valid, ct[...].astype(F32), 0.0)
        gs = norm_back(tangent * g2[...][None], xhat2[...], acc[:, 0:1])
        gnb[...] = gs.astype(BF)
        acc[...] = gs
        feed_back(gnb, wi, wt, a, dact, acc)
        gf1 = norm_back(acc[...] * g1[...][None], xhat1[...], r1s[...])
        acc[...] = gf1
        gfb = gf1.astype(BF)
        context_grad = nt(wo[...], gfb)
        for g in range(G):
            dot_ref[g] = context_grad[192 * g : 192 * g + 192]
        middle_sum = [jnp.zeros((16, S), F32)]
        first_rows = lax.broadcasted_iota(jnp.int32, (16, 192), 0) < 8

        def group_done(g):
            dqv = dyt[g]
            a[:, GW * g : GW * g + 384] = dqv.T
            gu = nt(mid[0:16, :], dqv)
            gu = jnp.where(first_rows, gu[:, 0:192], gu[:, 192:384]) * 2.0
            msg[g, 1, :, 256:512] = jnp.concatenate([gu, jnp.zeros((16, 64), F32)], axis=1).astype(BF)
            middle_sum[0] = middle_sum[0] + nn(up[g], dqv)

        attend_back([(g, j) for g in range(G) for j in range(3)], place, vnat, yt, p, rl, ctxt, dot_ref, dosc, dyt, group_done)
        gmb = middle_sum[0].astype(BF)
        gmid[0:16, :] = gmb
        gmid[16:64, :] = jnp.zeros((48, S), BF)
        gd = nn(gmb, x[...]).astype(BF)
        for g in range(G):
            msg[g, 0] = gd[:, 0:512]
            msg[g, 1, :, 0:256] = gd[:, 512:768]

    zsum = [
        remote(msg.at[i, turn2(ic, o)], redz.at[ic, iz], gz.at[0, o, i], gz.at[1, ic, iz], heads=turn(iz, i), dp_2=turn2(ic, o))
        for o in (0, 1) for i in range(4) if o + i > 0
    ]
    over_x = [
        remote(redx.at[ix], redx.at[ix], gx.at[0, i], gx.at[1, i], dp_0=turn(ix, i)) for i in (1, 2, 3)
    ]
    over_y = [
        remote(redy.at[ic, iy], redy.at[ic, iy], gy.at[0, o, i], gy.at[1, ic, iy], dp_1=turn(iy, i), dp_2=turn2(ic, o))
        for o in (0, 1) for i in range(4) if o + i > 0
    ]

    def start(copies):
        for c in copies:
            c.start()

    def finish_copies(copies):
        for c in copies:
            c.wait()

    def last_product(i):
        rows = pl.ds(pl.multiple_of(turn(rank, i) * Q, Q), Q)
        for g in range(G):
            dk = [nt(yt[g, 64 * j : 64 * j + 64, :], p[3 * g + j, rows, :]).astype(BF) for j in range(3)]
            tail = gmid[:, rows] if g == 0 else jnp.zeros((64, Q), BF)
            a[rows, GW * g + 384 : GW * g + GW] = jnp.concatenate(dk + [tail], axis=0).T
        igb[rows, :] = (acc[rows, :] + nn(a[rows, 0 : G * GW], wg[...])).astype(BF)
        if i:
            sent_back(igb, ig_out, isem, i).start()

    @pl.when(owner)
    def _():
        start(zsum)
        redz[ic, iz] = msg[0, ic]
        last_product(2)
        last_product(1)

    def from_others(buf, sem, c, n, me):
        @pl.when(jnp.logical_or(ic != c, me != n))
        def _():
            pltpu.make_async_copy(redx.at[0], buf.at[c, n], sem.at[1, c, n]).wait()

    total = jnp.zeros((16, 512), F32)
    for c in range(2):
        for z in range(4):
            if (z + 2 * c) % 4 != 3:
                from_others(redz, gz, c, z, iz)
                total = total + redz[c, z].astype(F32)
    redx[ix] = total.astype(BF)
    start(over_x)

    @pl.when(owner)
    def _():
        last_product(3)

    finish_copies(over_x)
    redy[ic, iy] = sum(redx[n].astype(F32) for n in range(4)).astype(BF)
    start(over_y)

    @pl.when(owner)
    def _():
        last_product(0)
        own_back(igb, ig_out, isem).start()

    halves = []
    for c in range(2):
        for n in range(4):
            from_others(redy, gy, c, n, iy)
        halves.append(sum(redy[c, n].astype(F32) for n in range(4)))
    gd_out[:, 0:512] = halves[0]
    gd_out[:, 512:768] = halves[1][:, 0:256]
    gu_out[...] = halves[1][:, 256:448]

    back_end(act, act_out, asem)
    back_end(igb, ig_out, isem)
    spread_end(cot, ct, csem)
    for c in ups:
        c.wait_send()

    weights_end()

    for c in over_y:
        c.wait_send()

    @pl.when(owner)
    def _():
        for c in zsum:
            c.wait_send()


def finish(act_in, ig_in, gd, gu, act, ig, gdq, guq, gdv, guv):
    act[...] = act_in[...]
    ig[...] = ig_in[...].astype(F32)
    gdq[...] = gd[0:8, :]
    gdv[...] = gd[8:16, :]
    guq[...] = gu[0:8, :]
    guv[...] = gu[8:16, :]


def scratch():
    V, dma = pltpu.VMEM, pltpu.SemaphoreType.DMA
    return [
        V((B, S), jnp.int32), V((D,), F32), V((D,), F32), V((D,), F32), V((D,), F32),
        V((8, D), BF), V((8, 192), BF), V((8, D), BF), V((8, 192), BF),
        V((S, D), BF), V((S, D), BF), V((D, D), BF), V((D, FF), BF), V((FF, D), BF), V((G * GW, D), BF),
        V((G, 16, 384), BF), V((S, D), BF), V((S, D), BF),
        V((64, S), BF), V((64, S), BF), V((G, S, 256), BF), V((G, S, 256), BF), V((G, GW, S), BF),
        V((3, S, 256), F32), V((12, S, S), BF), V((12, 1, S), F32), V((G, 192, S), BF),
        V((S, D), F32), V((S, D), F32), V((S, 1), F32), V((S, D), BF),
        V((2, S, C), F32), V((S, FF), BF), V((S, FF), F32), V((S, D), F32),
        V((G, 192, S), F32), V((3, 64, S), BF), V((G, 384, S), BF),
        V((S, D), BF),
        V((4, 2, 16, 512), BF), V((2, 4, 16, 512), BF), V((4, 16, 512), BF), V((2, 4, 16, 512), BF),
        V((64, S), BF),
        dma((15,)), dma((2, 4)), dma((2, 4)), dma((2, 4)), dma((2, 4)), dma((2, 4, 4)), dma((2, 4, 3, 4)), dma((2, 4)),
        dma((2, 4)), dma((2, 4)), dma((2, 2, 4)), dma((2, 4)), dma((2, 2, 4)),
    ]


def per_device(inputs, key_mask, lengths, cotangent, wq, wk, wv, w_out, w_inner, w_outer, g1, b1, g2, b2, dq, uq, dv, uv):
    vm, hbm = pl.BlockSpec(memory_space=pltpu.VMEM), pl.BlockSpec(memory_space=pl.ANY)
    shape = jax.ShapeDtypeStruct
    act, ig, gd, gu = pl.pallas_call(
        layer,
        out_shape=(shape((B, Q, D), BF), shape((B, Q, D), BF), shape((16, D), F32), shape((16, 192), F32)),
        in_specs=[hbm] * 3 + [pl.BlockSpec(memory_space=pltpu.SMEM)] + [hbm] * 14,
        out_specs=(hbm, hbm, vm, vm),
        scratch_shapes=scratch(),
        compiler_params=pltpu.CompilerParams(
            collective_id=0, has_side_effects=True, vmem_limit_bytes=62 * 2**20
        ),
    )(
        inputs, cotangent, key_mask, lengths, wq.T, wk.T, wv.T, w_out, w_inner, w_outer,
        g1, b1, g2, b2, dq.T, uq, dv.T, uv,
    )
    act, ig, gdq, guq, gdv, guv = pl.pallas_call(
        finish,
        out_shape=(
            shape((B, Q, D), BF), shape((B, Q, D), F32),
            shape((8, D), F32), shape((8, 192), F32), shape((8, D), F32), shape((8, 192), F32),
        ),
        in_specs=[vm] * 4,
        out_specs=(vm,) * 6,
    )(act, ig, gd, gu)
    return act, ig, gdq.T, guq, gdv.T, guv


def solution(mesh):
    finer = Mesh(
        mesh.devices.reshape(4, 4, 2, mesh.shape["heads"]), ("dp_0", "dp_1", "dp_2", "heads")
    )
    rows, cols, same = P(DP, "heads", None), P(None, "heads"), P()
    return jax.shard_map(
        per_device,
        mesh=finer,
        in_specs=(rows, P(DP, None), P(DP), rows, cols, cols, cols) + (same,) * 8 + (cols, same, cols),
        out_specs=(rows, rows, same, cols, same, cols),
        check_vma=False,
    )
```
